32 devices in a mesh: wide: 8 (over z, x), narrow: 4 (over y, core).
Axes of the slice: x: 2, y: 2, z: 4, core: 2. Of those that a mesh axis runs over, the one named last changes fastest.
Arguments:
- patches: bfloat16 [3200, 16384], P('wide', 'narrow')
- ln_gain: bfloat16 [4, 3200], P(None, 'wide'), may hold values from 0.5 to 1.5
- ln_bias: bfloat16 [4, 3200], P(None, 'wide'), may hold values from -3 to 3
- first_weight: bfloat16 [4, 3200, 6144], P(None, 'wide', 'narrow'), may hold values from -0.0546875 to 0.0546875
- first_bias: bfloat16 [6144], P('narrow'), may hold values from -3 to 3
- second_weight: bfloat16 [6144, 6144], P('wide', 'narrow'), may hold values from -0.078125 to 0.078125
- second_bias: bfloat16 [6144], P('wide'), may hold values from -3 to 3
- text_embeds: bfloat16 [6144, 5120], P('wide', 'narrow'), may hold values from -6 to 6
- vis_pos: int32 [4096], replicated, may hold values from 0 to 5119, as said below
Outputs:
- prompt_embeds: bfloat16 [6144, 5120], P('wide', 'narrow')
The draws below stay inside these ranges and needn't reach their ends.
Inputs may be any that keep to these rules, and one draw needn't show every extreme that they name: vis_pos is strictly increasing and made of runs of 256 consecutive prompt rows, one run per tile in tile order; the first visual row is the first prompt row and the last visual row is the last prompt row.
All inputs are finite; a program needn't handle non-finite values.
Results may differ from the reference program's by a relative error of at most 0.012.
Values may be sent and summed in bfloat16 or wider, within the bound.
No kernel may reach another device: no remote copies, remote signals or barrier semaphores. Data moves between devices by JAX's collectives and lax.ppermute only.
A program may use at most 128 MiB of HBM per device.

```python
import math
import jax
import jax.numpy as jnp
from jax import lax

D = 3200
E = 6144
TILE_SIDE = 32
TILE_ROWS = 256
TILES = 16
T_ROWS = 16384
VIS = 4096
TEXT = 1024
PROMPT = 5120


def draw_patches(key, part):
    first_key, second_key, third_key = jax.random.split(jax.random.fold_in(key, 11), 3)
    position = jnp.arange(D, dtype=jnp.float32) / D
    spread = jnp.exp(jax.random.uniform(second_key, (D,), jnp.float32, 0.0, math.log(10.0 / 3.0)))
    column = jnp.exp(position * math.log(3.0)) * spread
    base = jax.random.normal(first_key, (T_ROWS, D), jnp.float32)
    row_scale = jnp.exp(jax.random.uniform(third_key, (T_ROWS,), jnp.float32, 0.0, math.log(10.0)))
    return (base * row_scale[:, None] * column[None, :]).T.astype(jnp.bfloat16)


def draw_vis_pos(key, part):
    cut_key = jax.random.fold_in(key, 23)
    cuts = jax.random.randint(cut_key, (TILES,), 0, TEXT + 1)
    cuts = jnp.sort(cuts)
    cuts = cuts.at[0].set(0)
    cuts = cuts.at[TILES - 1].set(TEXT)
    starts = cuts + jnp.arange(TILES, dtype=jnp.int32) * TILE_ROWS
    offsets = jnp.arange(TILE_ROWS, dtype=jnp.int32)
    return (starts[:, None] + offsets[None, :]).reshape(VIS).astype(jnp.int32)


def block_scale(stream_key, dims, cuts, low, largest):
    def one(axis_at, shards_of):
        steps = jax.random.uniform(jax.random.fold_in(jax.random.fold_in(stream_key, 6), axis_at), (shards_of,), jnp.float32, low / len(cuts), largest / len(cuts))
        return jnp.repeat(jnp.exp(steps), dims[axis_at] // shards_of).reshape((-1,) + (1,) * (len(dims) - axis_at - 1))

    factor_of = one(*cuts[0])
    for cut in cuts[1:]:
        factor_of = factor_of * one(*cut)
    return factor_of


def centred(stream_key, dims, width, reach, cuts=(), kind=jnp.bfloat16):
    array = width * jax.random.normal(stream_key, dims, jnp.float32)
    if cuts:
        array = array * block_scale(stream_key, dims, cuts, -0.22, 0.18)
    return jnp.clip(array, -reach, reach).astype(kind)


def setup_inputs(seed: int = 0) -> dict:
    splits = jax.random.split(jax.random.key(seed), 10)
    patches = draw_patches(jax.random.fold_in(splits[9], 71), 0)
    ln_gain = jnp.clip(0.5 + 1.0 * jax.random.uniform(splits[1], (4, D), jnp.float32) ** block_scale(splits[1], (4, D), ((1, 8),), -0.2, 0.2), 0.5, 1.5).astype(jnp.bfloat16)
    ln_bias = centred(splits[2], (4, D), 0.5, 3.0, ((1, 8),))
    first_weight = centred(splits[3], (4, D, E), (4 * D) ** -0.5, 0.0546875, ((1, 8), (2, 4)))
    first_bias = centred(splits[4], (E,), 0.5, 3.0, ((0, 4),))
    second_weight = centred(splits[5], (E, E), E ** -0.5, 0.078125, ((0, 8), (1, 4)))
    second_bias = centred(splits[6], (E,), 0.5, 3.0, ((0, 8),))
    text_embeds = centred(splits[7], (E, PROMPT), 1.0, 6.0, ((0, 8), (1, 4)))
    vis_pos = draw_vis_pos(jax.random.fold_in(splits[9], 71), 0)
    return {"patches": patches, "ln_gain": ln_gain, "ln_bias": ln_bias, "first_weight": first_weight, "first_bias": first_bias, "second_weight": second_weight, "second_bias": second_bias, "text_embeds": text_embeds, "vis_pos": vis_pos}


def reference(patches, ln_gain, ln_bias, first_weight, first_bias, second_weight, second_bias, text_embeds, vis_pos):
    half_side = TILE_SIDE // 2
    patch_rows = patches.T
    merged = patch_rows.reshape(TILES, half_side, 2, half_side, 2, D).transpose(0, 1, 3, 2, 4, 5).reshape(VIS, 4, D)
    float_rows = merged.astype(jnp.float32)
    entries = 4.0 * D
    row_mean = lax.optimization_barrier(jnp.sum(float_rows, axis=(1, 2))) / entries
    row_var = lax.optimization_barrier(jnp.sum(float_rows * float_rows, axis=(1, 2))) / entries - row_mean * row_mean
    inverse = lax.rsqrt(row_var + 1e-05)
    normed = ((float_rows - row_mean[:, None, None]) * inverse[:, None, None] * ln_gain.astype(jnp.float32) + ln_bias.astype(jnp.float32)).astype(jnp.bfloat16)
    preact = jnp.dot(normed.reshape(VIS, 4 * D), first_weight.reshape(4 * D, E), preferred_element_type=jnp.float32)
    preact = preact + first_bias.astype(jnp.float32)
    activated = jax.nn.gelu(preact, approximate=False).astype(jnp.bfloat16)
    visual = jnp.dot(second_weight, activated.T, preferred_element_type=jnp.float32) + second_bias.astype(jnp.float32)[:, None]
    visual = visual.astype(jnp.bfloat16)
    return text_embeds.at[:, vis_pos.astype(jnp.int32)].set(visual)
```

```python
import jax
import jax.numpy as jnp
from jax import lax
from jax.experimental import pallas as pl
from jax.experimental.pallas import tpu as pltpu
from jax.sharding import PartitionSpec as P

D = 3200
TILE_SIDE = 32
TILE_ROWS = 256
HALF = 128
COLS = 512
F32 = jnp.float32
BF16 = jnp.bfloat16


def bit_reversed(bits):
    return [sum(((p >> b) & 1) << (bits - 1 - b) for b in range(bits)) for p in range(1 << bits)]


def swap(value, axis, mask):
    count = lax.axis_size(axis)
    return lax.ppermute(value, axis, [(i, i ^ mask) for i in range(count)])


def merge_kernel(patch_ref, order_ref, merged_ref, stats_ref):
    mixed = jnp.dot(patch_ref[...], order_ref[...], preferred_element_type=F32)
    total = jnp.zeros((1, HALF), F32)
    squares = jnp.zeros((1, HALF), F32)
    for slot in range(4):
        part = mixed[:, slot * HALF : (slot + 1) * HALF]
        merged_ref[0, slot] = part.astype(BF16)
        total += jnp.sum(part, axis=0, keepdims=True)
        squares += jnp.sum(part * part, axis=0, keepdims=True)
    stats_ref[0:1, :] = total
    stats_ref[1:2, :] = squares


def merge(patches):
    columns, width = patches.shape
    steps = width // COLS
    side = TILE_SIDE // 2
    source = lax.broadcasted_iota(jnp.int32, (COLS, COLS), 0)
    target = lax.broadcasted_iota(jnp.int32, (COLS, COLS), 1)
    slot = target // HALF
    row = target % HALF
    wanted = (
        (row // side) * (4 * side) + (slot // 2) * (2 * side) + (row % side) * 2 + slot % 2
    )
    order = (source == wanted).astype(BF16)
    return pl.pallas_call(
        merge_kernel,
        grid=(steps,),
        in_specs=[
            pl.BlockSpec((columns, COLS), lambda i: (0, i)),
            pl.BlockSpec((COLS, COLS), lambda i: (0, 0)),
        ],
        out_specs=[
            pl.BlockSpec((1, 4, columns, HALF), lambda i: (i, 0, 0, 0)),
            pl.BlockSpec((2, HALF), lambda i: (0, i)),
        ],
        out_shape=[
            jax.ShapeDtypeStruct((steps, 4, columns, HALF), BF16),
            jax.ShapeDtypeStruct((2, steps * HALF), F32),
        ],
        compiler_params=pltpu.CompilerParams(vmem_limit_bytes=32 * 1024 * 1024),
    )(patches, order)


def shards(
    patches,
    ln_gain,
    ln_bias,
    first_weight,
    first_bias,
    second_weight,
    second_bias,
    text_embeds,
    vis_pos,
):
    wide = lax.axis_size("wide")
    narrow = lax.axis_size("narrow")
    wide_bits = wide.bit_length() - 1
    narrow_bits = narrow.bit_length() - 1
    wide_at = lax.axis_index("wide")
    narrow_at = lax.axis_index("narrow")
    side_at = wide_at % 2
    column_at = wide_at // 2
    columns = patches.shape[0]
    hidden = first_weight.shape[2]
    features = second_weight.shape[0]
    tiles = patches.shape[1] // (4 * TILE_ROWS)
    prompt_rows = text_embeds.shape[1]
    depth = 4 * columns

    unit_order = bit_reversed(wide_bits - 1)
    block = hidden // len(unit_order)
    starts = [(q ^ column_at) * block for q in unit_order]
    flat_weight = first_weight.reshape(depth, hidden)
    first = jnp.concatenate(
        [lax.dynamic_slice_in_dim(flat_weight, s, block, 1).T for s in starts], axis=0
    )
    own_bias = lax.dynamic_slice_in_dim(first_bias, starts[0], block, 0).astype(F32)[:, None]
    second_own = jnp.concatenate(
        [lax.dynamic_slice_in_dim(second_weight, s, block, 1) for s in starts], axis=1
    )
    second_other = swap(second_own, "wide", 1)
    second = jnp.concatenate([second_other, second_own], axis=0)
    out_bias = jnp.concatenate([swap(second_bias, "wide", 1), second_bias]).astype(F32)[:, None]

    merged, stats = merge(patches)
    for bit in range(wide_bits):
        stats = stats + swap(stats, "wide", 1 << bit)
    entries = 4.0 * D
    row_mean = stats[0] / entries
    row_var = stats[1] / entries - row_mean * row_mean
    inverse = lax.rsqrt(row_var + 1e-05)
    gain = ln_gain.astype(F32)[:, :, None]
    shift = ln_bias.astype(F32)[:, :, None]

    def normed(half):
        values = lax.dynamic_index_in_dim(merged, half, 0, keepdims=False).astype(F32)
        mean = lax.dynamic_slice_in_dim(row_mean, half * HALF, HALF, 0)
        scale = lax.dynamic_slice_in_dim(inverse, half * HALF, HALF, 0)
        result = (values - mean[None, None, :]) * scale[None, None, :] * gain + shift
        return result.astype(BF16).reshape(depth, HALF)

    tile_order = bit_reversed(narrow_bits)

    def gathered(own):
        found = {0: own}
        for bit in reversed(range(narrow_bits)):
            for d in list(found):
                found[d ^ (1 << bit)] = swap(found[d], "narrow", 1 << bit)
        return jnp.concatenate([found[d] for d in tile_order], axis=1)

    finals = []
    for tile in range(tiles):
        theirs = gathered(normed(2 * tile + 1 - side_at))
        mine = gathered(normed(2 * tile + side_at))
        sent = jnp.dot(first, theirs, preferred_element_type=F32).astype(BF16)
        came = swap(sent, "wide", 1)
        total = jnp.dot(first, mine, preferred_element_type=F32) + came.astype(F32)
        for bit in range(1, wide_bits):
            total = total.astype(BF16)
            cut = total.shape[0] // 2
            came = swap(total[cut:], "wide", 1 << bit)
            total = total[:cut].astype(F32) + came.astype(F32)
        activated = jax.nn.gelu(total + own_bias, approximate=False).astype(BF16)
        pieces = [activated]
        for bit in reversed(range(1, wide_bits)):
            pieces = pieces + [swap(piece, "wide", 1 << bit) for piece in pieces]
        units = jnp.concatenate(pieces, axis=0)
        value = jnp.dot(second, units, preferred_element_type=F32)
        for bit in range(narrow_bits):
            value = value.astype(BF16)
            cut = value.shape[1] // 2
            came = swap(value[:, cut:], "narrow", 1 << bit)
            value = value[:, :cut].astype(F32) + came.astype(F32)
        visual = (value + out_bias).astype(BF16)
        other = swap(visual[:features], "wide", 1)
        finals.append(jnp.concatenate([visual[features:], other], axis=1))

    text_rows = narrow * prompt_rows - vis_pos.shape[0]
    first_row = narrow_at * prompt_rows
    half_rows = jnp.arange(HALF, dtype=jnp.int32)
    in_tile = jnp.concatenate([half_rows + side_at * HALF, half_rows + (1 - side_at) * HALF])
    placed, spots = [], []
    for step in range(1 - narrow, narrow):
        for tile in range(tiles):
            pairs = []
            for source in range(narrow):
                target = source + step
                low = (source * tiles + tile) * TILE_ROWS
                if (
                    0 <= target < narrow
                    and low < (target + 1) * prompt_rows
                    and low + text_rows + TILE_ROWS > target * prompt_rows
                ):
                    pairs.append((source, target))
            if not pairs:
                continue
            placed.append(finals[tile] if step == 0 else lax.ppermute(finals[tile], "narrow", pairs))
            whose = narrow_at - step
            at = (jnp.clip(whose, 0, narrow - 1) * tiles + tile) * TILE_ROWS
            spot = lax.dynamic_slice_in_dim(vis_pos, at, TILE_ROWS, 0)[in_tile] - first_row
            spots.append(jnp.where((whose >= 0) & (whose < narrow), spot, -1))
    spot = jnp.concatenate(spots)
    grid = jnp.arange(prompt_rows, dtype=jnp.int32)[None, :]
    hits = spot[:, None] == grid
    marked = jnp.any(hits, axis=0)
    moved = jnp.dot(
        jnp.concatenate(placed, axis=1), hits.astype(BF16), preferred_element_type=F32
    ).astype(BF16)
    return jnp.where(marked[None, :], moved, text_embeds)


def solution(mesh):
    in_specs = (
        P("wide", "narrow"),
        P(None, "wide"),
        P(None, "wide"),
        P(None, "wide", "narrow"),
        P("narrow"),
        P("wide", "narrow"),
        P("wide"),
        P("wide", "narrow"),
        P(),
    )
    out_specs = P("wide", "narrow")
    return jax.shard_map(shards, mesh=mesh, in_specs=in_specs, out_specs=out_specs, check_vma=False)
```

```python
import functools

import jax
import jax.numpy as jnp
from jax import lax
from jax.experimental import pallas as pl
from jax.experimental.pallas import tpu as pltpu
from jax.sharding import PartitionSpec as P

D = 3200
TILE_SIDE = 32
TILE_ROWS = 256
HALF = 128
COLS = 512
F32 = jnp.float32
BF16 = jnp.bfloat16


def bit_reversed(bits):
    return [sum(((p >> b) & 1) << (bits - 1 - b) for b in range(bits)) for p in range(1 << bits)]


def swap(value, axis, mask):
    count = lax.axis_size(axis)
    return lax.ppermute(value, axis, [(i, i ^ mask) for i in range(count)])


def merge_kernel(patch_ref, order_ref, merged_ref, stats_ref):
    mixed = jnp.dot(patch_ref[...], order_ref[...], preferred_element_type=F32)
    total = jnp.zeros((1, HALF), F32)
    squares = jnp.zeros((1, HALF), F32)
    for slot in range(4):
        part = mixed[:, slot * HALF : (slot + 1) * HALF]
        merged_ref[0, slot] = part.astype(BF16)
        total += jnp.sum(part, axis=0, keepdims=True)
        squares += jnp.sum(part * part, axis=0, keepdims=True)
    stats_ref[0:1, :] = total
    stats_ref[1:2, :] = squares


def merge(patches):
    columns, width = patches.shape
    steps = width // COLS
    side = TILE_SIDE // 2
    source = lax.broadcasted_iota(jnp.int32, (COLS, COLS), 0)
    target = lax.broadcasted_iota(jnp.int32, (COLS, COLS), 1)
    slot = target // HALF
    row = target % HALF
    wanted = (
        (row // side) * (4 * side) + (slot // 2) * (2 * side) + (row % side) * 2 + slot % 2
    )
    order = (source == wanted).astype(BF16)
    return pl.pallas_call(
        merge_kernel,
        grid=(steps,),
        in_specs=[
            pl.BlockSpec((columns, COLS), lambda i: (0, i)),
            pl.BlockSpec((COLS, COLS), lambda i: (0, 0)),
        ],
        out_specs=[
            pl.BlockSpec((1, 4, columns, HALF), lambda i: (i, 0, 0, 0)),
            pl.BlockSpec((2, HALF), lambda i: (0, i)),
        ],
        out_shape=[
            jax.ShapeDtypeStruct((steps, 4, columns, HALF), BF16),
            jax.ShapeDtypeStruct((2, steps * HALF), F32),
        ],
        compiler_params=pltpu.CompilerParams(vmem_limit_bytes=32 * 1024 * 1024),
    )(patches, order)


def shards(
    patches,
    ln_gain,
    ln_bias,
    first_weight,
    first_bias,
    second_weight,
    second_bias,
    text_embeds,
    vis_pos,
):
    wide = lax.axis_size("wide")
    narrow = lax.axis_size("narrow")
    wide_bits = wide.bit_length() - 1
    narrow_bits = narrow.bit_length() - 1
    line = wide // 2
    wide_at = lax.axis_index("wide")
    narrow_at = lax.axis_index("narrow")
    side_at = wide_at % 2
    line_at = wide_at // 2
    columns = patches.shape[0]
    hidden = first_weight.shape[2]
    features = second_weight.shape[0]
    tiles = patches.shape[1] // (4 * TILE_ROWS)
    prompt_rows = text_embeds.shape[1]
    depth = 4 * columns
    block = hidden // line

    merged, stats = merge(patches)
    other_bias = swap(second_bias, "wide", 1)
    stats = stats + swap(stats, "wide", 1)
    stats, second_sent, other_bias = lax.optimization_barrier((stats, second_weight, other_bias))
    early = features // 3 // 16 * 16
    for bit in range(1, wide_bits):
        stats = stats + swap(stats, "wide", 1 << bit)
    entries = 4.0 * D
    row_mean = stats[0] / entries
    row_var = stats[1] / entries - row_mean * row_mean
    inverse = lax.rsqrt(row_var + 1e-05)
    gain = ln_gain.astype(F32)[:, :, None]
    shift = ln_bias.astype(F32)[:, :, None]

    def normed(half):
        values = lax.dynamic_index_in_dim(merged, half, 0, keepdims=False).astype(F32)
        mean = lax.dynamic_slice_in_dim(row_mean, half * HALF, HALF, 0)
        scale = lax.dynamic_slice_in_dim(inverse, half * HALF, HALF, 0)
        result = (values - mean[None, None, :]) * scale[None, None, :] * gain + shift
        return result.astype(BF16).reshape(depth, HALF)

    if line == 4:
        starts = [(line_at // 2 ^ i) * (hidden // 2) for i in range(2)]
    else:
        starts = [(line_at ^ i) * (hidden // line) for i in bit_reversed(wide_bits - 1)]
    block = hidden // len(starts)
    flat = first_weight.reshape(depth, hidden)
    own_bias = lax.dynamic_slice_in_dim(first_bias, starts[0], block, 0).astype(F32)[:, None]
    out_bias = jnp.concatenate([second_bias, other_bias]).astype(F32)[:, None]

    text_rows = narrow * prompt_rows - vis_pos.shape[0]
    first_row = narrow_at * prompt_rows
    grid = jnp.arange(prompt_rows, dtype=jnp.int32)[None, :]
    moves = {tile: [] for tile in range(tiles)}
    hits = {}
    for tile in range(tiles):
        spots = []
        for step in range(1 - narrow, narrow):
            pairs = []
            for source in range(narrow):
                target = source + step
                low = (source * tiles + tile) * TILE_ROWS
                if (
                    0 <= target < narrow
                    and low < (target + 1) * prompt_rows
                    and low + text_rows + TILE_ROWS > target * prompt_rows
                ):
                    pairs.append((source, target))
            if not pairs:
                continue
            moves[tile].append((step, pairs))
            whose = narrow_at - step
            at = (jnp.clip(whose, 0, narrow - 1) * tiles + tile) * TILE_ROWS
            spot = jnp.concatenate(
                [
                    lax.dynamic_slice_in_dim(vis_pos, at + half * HALF, HALF, 0) - first_row
                    for half in (side_at, 1 - side_at)
                ]
            )
            spots.append(jnp.where((whose >= 0) & (whose < narrow), spot, -1))
        hits[tile] = jnp.concatenate(spots)[:, None] == grid
    marked = functools.reduce(jnp.logical_or, [jnp.any(h, axis=0) for h in hits.values()])

    tile_order = bit_reversed(narrow_bits)
    outward = [(x, 2 + x) for x in (0, 1)] + [(6 + x, 4 + x) for x in (0, 1)]
    inward = [(b, a) for a, b in outward]
    middle = [(2 + x, 4 + x) for x in (0, 1)] + [(4 + x, 2 + x) for x in (0, 1)]
    is_middle = (line_at == 1) | (line_at == 2)
    have, joined = {}, set()

    def put(key, value, flying=False):
        have[key] = value
        joined.discard(key)
        if not flying:
            joined.add(key)

    def fly(key, value, axis, pairs):
        if isinstance(pairs, int):
            pairs = [(i, i ^ pairs) for i in range(lax.axis_size(axis))]
        put(key, lax.ppermute(value, axis, pairs), True)
        put(("sent", key), value)

    def sync(needs):
        joined.update(needs)
        keys = [k for k in have if k in joined]
        have.update(zip(keys, lax.optimization_barrier([have[k] for k in keys])))
        for key in keys:
            if key[0] == "sent":
                del have[key]

    def gather_step(key, tile, bits):
        if bits[0] == narrow_bits - 1:
            theirs, mine = normed_halves[tile]
            own = {"theirs": [theirs], "mine": [mine], "both": [theirs, mine]}[key]
            put((key, 0, tile), jnp.concatenate(own, axis=1))
        for bit in bits:
            for d in range(narrow):
                if d % (2 << bit) == 0:
                    fly((key, d + (1 << bit), tile), have[key, d, tile], "narrow", 1 << bit)

    def rows_of(key, tile):
        if (key, 0, tile) in have:
            return jnp.concatenate([have.pop((key, d, tile)) for d in tile_order], axis=1)
        at = 0 if key == "theirs" else HALF
        return jnp.concatenate(
            [have["both", d, tile][:, at : at + HALF] for d in tile_order], axis=1
        )

    def first_product(rows):
        return lax.dot_general(have["first",], rows, (((0,), (0,)), ((), ())), preferred_element_type=F32)

    def send_theirs(tile):
        sent = first_product(rows_of("theirs", tile)).astype(BF16)
        fly(("came", tile), sent, "wide", 1)

    def keep_mine(tile):
        put(("own", tile), first_product(rows_of("mine", tile)))
        for d in range(narrow):
            have.pop(("both", d, tile), None)

    def second_columns(at):
        parts = [second_weight, have["second", 0], have["second", 1]]
        return jnp.concatenate(
            [lax.dynamic_slice_in_dim(part, at, block, 1) for part in parts], axis=0
        )

    def far_out(tile):
        own, came = have.pop(("own", tile)), have.pop(("came", tile))
        far = (own[block:] + came[block:].astype(F32)).astype(BF16)
        put(("far", tile), far)
        fly(("far_came", tile), far, "wide", outward)
        near = (own[:block] + came[:block].astype(F32)).astype(BF16)
        put(("near", tile), near)
        fly(("near_came", tile), near, "wide", outward)

    def across(tile):
        far = have.pop(("far", tile)).astype(F32) + have.pop(("far_came", tile)).astype(F32)
        fly(("across", tile), far.astype(BF16), "wide", middle)

    def activate(tile):
        total = have.pop(("near", tile)).astype(F32) + have.pop(("near_came", tile)).astype(F32)
        total = total + have.pop(("across", tile)).astype(F32)
        act = jax.nn.gelu(total + own_bias, approximate=False).astype(BF16)
        put(("act", tile), act)
        fly(("far_act", tile), act, "wide", middle)
        fly(("near_act", tile), act, "wide", inward)

    def far_in(tile):
        fly(("far_act_end", tile), have["far_act", tile], "wide", inward)
        near = jnp.where(is_middle, have.pop(("act", tile)), have.pop(("near_act", tile)))
        put(("near_units", tile), near)

    def near_product(tile):
        near = have.pop(("near_units", tile))
        put(("value", tile), jnp.dot(second_columns(starts[0]), near, preferred_element_type=F32))

    def second_product(tile):
        if line == 4:
            far = have.pop(("far_act", tile)) + have.pop(("far_act_end", tile))
            more = jnp.dot(second_columns(starts[1]), far, preferred_element_type=F32)
            put(("value", tile), have["value", tile] + more)
        else:
            units = jnp.concatenate(have.pop(("acts", tile)), axis=0)
            second = jnp.concatenate([second_columns(s) for s in starts], axis=1)
            put(("value", tile), jnp.dot(second, units, preferred_element_type=F32))
        narrow_step(tile, 0)

    def halve(bit):
        def step(tile):
            if bit == 1:
                total = have.pop(("own", tile)) + have.pop(("came", tile)).astype(F32)
            else:
                total = have.pop(("sum", tile)).astype(F32) + have.pop(("part", tile)).astype(F32)
            total = total.astype(BF16)
            cut = total.shape[0] // 2
            put(("sum", tile), total[:cut])
            put(("part", tile), swap(total[cut:], "wide", 1 << bit))

        return step

    def double(bit):
        def step(tile):
            if bit == wide_bits - 1:
                total = have.pop(("sum", tile)).astype(F32) + have.pop(("part", tile)).astype(F32)
                act = jax.nn.gelu(total + own_bias, approximate=False).astype(BF16)
                put(("acts", tile), [act])
            acts = have["acts", tile]
            put(("acts", tile), acts + [swap(act, "wide", 1 << bit) for act in acts])

        return step

    def narrow_step(tile, bit):
        value = have["value", tile]
        if bit:
            value = value.astype(F32) + have["part", tile].astype(F32)
        value = value.astype(BF16)
        cut = value.shape[1] // 2
        fly(("part", tile), value[:, cut:], "narrow", 1 << bit)
        put(("value", tile), value[:, :cut])

    def trade(tile):
        value = have.pop(("value", tile)).astype(F32) + have.pop(("part", tile)).astype(F32)
        visual = (value + out_bias).astype(BF16)
        put(("kept", tile), visual[:features])
        fly(("traded", tile), visual[features:], "wide", 1)

    def halo(tile):
        whole = jnp.concatenate([have.pop(("kept", tile)), have.pop(("traded", tile))], axis=1)
        for step, pairs in moves[tile]:
            if step:
                fly(("moved", step, tile), whole, "narrow", pairs)
            else:
                put(("moved", step, tile), whole)

    def place(tile):
        moved = jnp.concatenate([have.pop(("moved", step, tile)) for step, _ in moves[tile]], axis=1)
        more = jnp.dot(moved, hits[tile].astype(BF16), preferred_element_type=F32)
        put(("placed",), have["placed",] + more.astype(BF16))

    def late_second():
        fly(("second", 1), have.pop(("second_late",))[early:], "wide", 1)

    def order_first():
        flat = have["first",]
        cut = [lax.dynamic_slice_in_dim(flat, s, block, 1) for s in starts]
        put(("first",), jnp.concatenate(cut, axis=1))

    def clear_marked():
        put(("placed",), jnp.where(marked[None, :], jnp.zeros((), BF16), have["placed",]))

    normed_halves = {
        tile: (normed(2 * tile + 1 - side_at), normed(2 * tile + side_at)) for tile in range(tiles)
    }
    high, low = [narrow_bits - 1], list(reversed(range(narrow_bits - 1)))
    put(("first",), flat)
    put(("placed",), text_embeds)
    put(("second_late",), second_sent)
    fly(("second", 0), second_sent[:early], "wide", 1)

    events = []

    def at(time, needs, step, *args):
        events.append((time, len(events), needs, step, args))

    def of(key, tile, bits):
        return [(key, d + (1 << b), tile) for b in bits for d in range(narrow) if d % (2 << b) == 0]

    at(20, [], gather_step, "theirs", 0, high)
    at(21, [], gather_step, "mine", 0, high)
    at(22, [], order_first)
    at(30, of("theirs", 0, high), gather_step, "theirs", 0, low)
    at(31, [], gather_step, "both", 1, high)
    at(34, of("theirs", 0, low) + [("second", 0)], send_theirs, 0)
    at(40, of("mine", 0, high), gather_step, "mine", 0, low)
    at(41, [], clear_marked)
    at(46, of("mine", 0, low), keep_mine, 0)
    at(60, of("both", 1, high), gather_step, "both", 1, low)
    at(61, [], gather_step, "both", 2, high)
    at(64, of("both", 1, low), send_theirs, 1)
    for tile in range(tiles):
        base = 82 + 38 * tile
        late = 82 + 38 * (tiles - 1) + 38
        if line == 4:
            at(base, [("came", tile)], far_out, tile)
            at(base + 21, [("far_came", tile)], across, tile)
            at(base + 44, [("across", tile), ("near_came", tile)], activate, tile)
            at(base + 67, [("far_act", tile), ("near_act", tile)], far_in, tile)
            at(max(base + 68, late + tile), [("second", 1)], near_product, tile)
            ready = max(base + 90, late + 2 + tile)
            at(ready, [("far_act_end", tile)], second_product, tile)
        else:
            for i, bit in enumerate(range(1, wide_bits)):
                at(base + 10 * i, [("part", tile)] if i else [("came", tile)], halve(bit), tile)
            for i, bit in enumerate(reversed(range(1, wide_bits))):
                needs = [] if i else [("part", tile)]
                at(base + 45 + 10 * i, needs, double(bit), tile)
            ready = max(base + 90, late + 2 + tile)
            at(ready, [("second", 1)], second_product, tile)
        for bit in range(1, narrow_bits):
            at(ready + 4 * bit, [("part", tile)], narrow_step, tile, bit)
        after = ready + 4 * narrow_bits + 9
        at(after, [("part", tile)], trade, tile)
        at(after + 8, [("traded", tile)], halo, tile)
        flown = [("moved", step, tile) for step, _ in moves[tile] if step]
        at(after + 16, flown, place, tile)
        if tile + 1 < tiles:
            at(base + 32, [], keep_mine, tile + 1)
        if tile + 2 < tiles:
            at(base + 9, of("both", tile + 2, high), gather_step, "both", tile + 2, low)
            at(base + 14, of("both", tile + 2, low), send_theirs, tile + 2)
        if tile + 3 < tiles:
            at(base + 10, [], gather_step, "both", tile + 3, high)
    at(82 + 38 * (tiles - 3) + 15, [], late_second)
    for _, _, needs, step, args in sorted(events, key=lambda e: e[:2]):
        sync(needs)
        step(*args)
    return have["placed",]


def solution(mesh):
    in_specs = (
        P("wide", "narrow"),
        P(None, "wide"),
        P(None, "wide"),
        P(None, "wide", "narrow"),
        P("narrow"),
        P("wide", "narrow"),
        P("wide"),
        P("wide", "narrow"),
        P(),
    )
    out_specs = P("wide", "narrow")
    return jax.shard_map(shards, mesh=mesh, in_specs=in_specs, out_specs=out_specs, check_vma=False)
```

```python
import functools

import jax
import jax.numpy as jnp
from jax import lax
from jax.experimental import pallas as pl
from jax.experimental.pallas import tpu as pltpu
from jax.sharding import PartitionSpec as P

D = 3200
TILE_SIDE = 32
TILE_ROWS = 256
HALF = 128
COLS = 512
F32 = jnp.float32
BF16 = jnp.bfloat16


def bit_reversed(bits):
    return [sum(((p >> b) & 1) << (bits - 1 - b) for b in range(bits)) for p in range(1 << bits)]


def swap(value, axis, mask):
    count = lax.axis_size(axis)
    return lax.ppermute(value, axis, [(i, i ^ mask) for i in range(count)])


def merge_kernel(patch_ref, order_ref, merged_ref, stats_ref):
    mixed = jnp.dot(patch_ref[...], order_ref[...], preferred_element_type=F32)
    total = jnp.zeros((1, HALF), F32)
    squares = jnp.zeros((1, HALF), F32)
    for slot in range(4):
        part = mixed[:, slot * HALF : (slot + 1) * HALF]
        merged_ref[0, slot] = part.astype(BF16)
        total += jnp.sum(part, axis=0, keepdims=True)
        squares += jnp.sum(part * part, axis=0, keepdims=True)
    stats_ref[0:1, :] = total
    stats_ref[1:2, :] = squares


def merge(patches):
    columns, width = patches.shape
    steps = width // COLS
    side = TILE_SIDE // 2
    source = lax.broadcasted_iota(jnp.int32, (COLS, COLS), 0)
    target = lax.broadcasted_iota(jnp.int32, (COLS, COLS), 1)
    slot = target // HALF
    row = target % HALF
    wanted = (
        (row // side) * (4 * side) + (slot // 2) * (2 * side) + (row % side) * 2 + slot % 2
    )
    order = (source == wanted).astype(BF16)
    return pl.pallas_call(
        merge_kernel,
        grid=(steps,),
        in_specs=[
            pl.BlockSpec((columns, COLS), lambda i: (0, i)),
            pl.BlockSpec((COLS, COLS), lambda i: (0, 0)),
        ],
        out_specs=[
            pl.BlockSpec((1, 4, columns, HALF), lambda i: (i, 0, 0, 0)),
            pl.BlockSpec((2, HALF), lambda i: (0, i)),
        ],
        out_shape=[
            jax.ShapeDtypeStruct((steps, 4, columns, HALF), BF16),
            jax.ShapeDtypeStruct((2, steps * HALF), F32),
        ],
        compiler_params=pltpu.CompilerParams(vmem_limit_bytes=16 * 1024 * 1024),
    )(patches, order)


def call(kernel, grid, in_specs, out_specs, out_shape, scratch_shapes=(), scalars=0, flops=1):
    return pl.pallas_call(
        kernel,
        grid_spec=pltpu.PrefetchScalarGridSpec(
            num_scalar_prefetch=scalars,
            grid=grid,
            in_specs=in_specs,
            out_specs=out_specs,
            scratch_shapes=scratch_shapes,
        ),
        out_shape=out_shape,
        cost_estimate=pl.CostEstimate(flops=flops, bytes_accessed=1, transcendentals=0),
        compiler_params=pltpu.CompilerParams(vmem_limit_bytes=16 * 1024 * 1024),
    )


def like(rows, width):
    return jax.ShapeDtypeStruct((rows, width), BF16)


def norm_kernel(half_ref, merged_ref, mean_ref, scale_ref, gain_ref, shift_ref, *out_refs):
    slots = 4 // len(out_refs)
    for slot in range(4):
        values = merged_ref[0, slot].astype(F32)
        gain, shift = gain_ref[:, slot : slot + 1], shift_ref[:, slot : slot + 1]
        result = (values - mean_ref[...]) * scale_ref[...] * gain + shift
        out_refs[slot // slots][slot % slots] = result.astype(BF16)


def norm(merged, mean, scale, gain, shift, halves):
    columns = merged.shape[2]
    count = 2 if columns % 16 == 0 else 1
    out = call(
        norm_kernel,
        (len(halves),),
        [
            pl.BlockSpec((1, 4, columns, HALF), lambda i, h: (h[i], 0, 0, 0)),
            pl.BlockSpec((1, HALF), lambda i, h: (0, h[i])),
            pl.BlockSpec((1, HALF), lambda i, h: (0, h[i])),
            pl.BlockSpec((columns, 4), lambda i, h: (0, 0)),
            pl.BlockSpec((columns, 4), lambda i, h: (0, 0)),
        ],
        [pl.BlockSpec((4 // count, columns, HALF), lambda i, h: (0, 0, i))] * count,
        [jax.ShapeDtypeStruct((4 // count, columns, len(halves) * HALF), BF16)] * count,
        scalars=1,
    )(jnp.stack(halves).astype(jnp.int32), merged, mean, scale, gain, shift)
    return [part.reshape(-1, len(halves) * HALF) for part in out]


def turn_kernel(first_ref, flat_ref, out_ref):
    out_ref[...] = flat_ref[...].T


def turn(flat, near):
    depth, hidden = flat.shape
    step = 256
    half = hidden // 2 // step
    return call(
        turn_kernel,
        (2 * half,),
        [pl.BlockSpec((depth, step), lambda i, n: (0, (i // half + n[0]) % 2 * half + i % half))],
        pl.BlockSpec((step, depth), lambda i, n: (i, 0)),
        like(hidden, depth),
        scalars=1,
    )(near, flat)


def stage(rows_ref, tile_refs, columns, places):
    for parts, place in zip(tile_refs, places):
        row = 0
        for part in parts:
            rows_ref[row : row + part.shape[0], place : place + HALF] = part[:, columns]
            row += part.shape[0]


def by_tile(refs, count):
    return [refs[i : i + count] for i in range(0, len(refs), count)]


def product_kernel(count, weight_ref, *refs):
    tile_refs, out_ref, rows_ref = by_tile(refs[:-2], count), refs[-2], refs[-1]

    @pl.when(pl.program_id(0) == 0)
    def _():
        places = [i * HALF for i in range(len(tile_refs))]
        stage(rows_ref, tile_refs, slice(None), places)

    out = jnp.dot(weight_ref[...], rows_ref[...], preferred_element_type=F32)
    out_ref[...] = out.astype(out_ref.dtype)


def product(weight, tiles, half, start, rows):
    depth = weight.shape[1]
    step = 256 if rows % 256 == 0 else rows
    width = len(tiles) * HALF
    parts = [part for tile in tiles for part in tile]
    return call(
        functools.partial(product_kernel, len(tiles[0])),
        (rows // step,),
        [pl.BlockSpec((step, depth), lambda i: (i + start // step, 0))]
        + [pl.BlockSpec((part.shape[0], HALF), lambda i: (0, half)) for part in parts],
        pl.BlockSpec((step, width), lambda i: (i, 0)),
        like(rows, width),
        [pltpu.VMEM((depth, width), BF16)],
    )(weight, *parts)


def products_kernel(count, weight_ref, *refs):
    tile_refs, (near_ref, far_ref, own_ref, rows_ref) = by_tile(refs[:-4], count), refs[-4:]
    width = len(tile_refs) * HALF
    step = pl.program_id(0)
    half = pl.num_programs(0) // 2

    @pl.when(step == 0)
    def _():
        places = [i * HALF for i in range(len(tile_refs))]
        stage(rows_ref, tile_refs, slice(0, HALF), places)
        stage(rows_ref, tile_refs, slice(HALF, 2 * HALF), [width + place for place in places])

    out = jnp.dot(weight_ref[...], rows_ref[...], preferred_element_type=F32).astype(BF16)
    own_ref[...] = out[:, width:]

    @pl.when(step < half)
    def _():
        near_ref[...] = out[:, :width]

    @pl.when(step >= half)
    def _():
        far_ref[...] = out[:, :width]


def products(weight, tiles):
    rows, depth = weight.shape
    step = 256
    half = rows // step // 2
    width = len(tiles) * HALF
    parts = [part for tile in tiles for part in tile]
    return call(
        functools.partial(products_kernel, len(tiles[0])),
        (2 * half,),
        [pl.BlockSpec((step, depth), lambda i: (i, 0))]
        + [pl.BlockSpec((part.shape[0], 2 * HALF), lambda i: (0, 0)) for part in parts],
        [
            pl.BlockSpec((step, width), lambda i: (jnp.minimum(i, half - 1), 0)),
            pl.BlockSpec((step, width), lambda i: (jnp.maximum(i - half, 0), 0)),
            pl.BlockSpec((step, width), lambda i: (i, 0)),
        ],
        [like(rows // 2, width), like(rows // 2, width), like(rows, width)],
        [pltpu.VMEM((depth, 2 * width), BF16)],
    )(weight, *parts)


def add_kernel(one_ref, other_ref, out_ref):
    out_ref[...] = (one_ref[...].astype(F32) + other_ref[...].astype(F32)).astype(BF16)


def add(one, other, start=0):
    rows, width = other.shape
    step = rows // 2
    spec = pl.BlockSpec((step, width), lambda i: (i, 0))
    one_spec = pl.BlockSpec((step, width), lambda i: (i + start // step, 0))
    return call(add_kernel, (2,), [one_spec, spec], spec, like(rows, width))(one, other)


def activate_kernel(one_ref, two_ref, three_ref, bias_ref, out_ref):
    total = one_ref[...].astype(F32) + two_ref[...].astype(F32) + three_ref[...].astype(F32)
    total = total + bias_ref[...]
    out_ref[...] = (0.5 * total * (1.0 + lax.erf(total * 0.5**0.5))).astype(BF16)


def activated_sum(one, two, three, bias):
    rows, width = one.shape
    step = rows // 4
    spec = pl.BlockSpec((step, width), lambda i: (i, 0))
    bias_spec = pl.BlockSpec((step, 1), lambda i: (i, 0))
    return call(
        activate_kernel, (4,), [spec, spec, spec, bias_spec], spec, like(rows, width)
    )(one, two, three, bias)


def put_halves(out, keep_refs, send_refs):
    half = pl.num_programs(0) // 2
    cut = out.shape[1] // 2
    for i in range(2):

        @pl.when((pl.program_id(0) >= half) if i else (pl.program_id(0) < half))
        def _():
            keep_refs[i][...] = out[:, :cut].astype(BF16)
            send_refs[i][...] = out[:, cut:].astype(BF16)


def halves_specs(step, half, cut):
    first = pl.BlockSpec((step, cut), lambda i, p: (jnp.minimum(i, half - 1), 0))
    last = pl.BlockSpec((step, cut), lambda i, p: (jnp.maximum(i - half, 0), 0))
    return [first, last, first, last]


def second_kernel(place_ref, near_weight_ref, far_weight_ref, *refs):
    own_ref, near_ref, far_ref, end_ref, keep_0, keep_1, send_0, send_1, units_ref = refs
    half = near_weight_ref.shape[1]

    @pl.when((pl.program_id(0) == 0) & (place_ref[1] == 1))
    def _():
        units_ref[:half, :] = own_ref[...]
        units_ref[half:, :] = far_ref[...]

    @pl.when((pl.program_id(0) == 0) & (place_ref[1] == 0))
    def _():
        units_ref[:half, :] = near_ref[...]
        units_ref[half:, :] = end_ref[...]

    out = jnp.dot(near_weight_ref[...], units_ref[:half, :], preferred_element_type=F32)
    out += jnp.dot(far_weight_ref[...], units_ref[half:, :], preferred_element_type=F32)
    put_halves(out, (keep_0, keep_1), (send_0, send_1))


def second_product_of(place, weight, own, near, far, end):
    rows, depth = weight.shape
    width = own.shape[1]
    step = 256
    unit_spec = pl.BlockSpec((depth // 2, width), lambda i, p: (0, 0))
    return call(
        second_kernel,
        (rows // step,),
        [
            pl.BlockSpec((step, depth // 2), lambda i, p: (i, p[0])),
            pl.BlockSpec((step, depth // 2), lambda i, p: (i, 1 - p[0])),
        ]
        + [unit_spec] * 4,
        halves_specs(step, rows // step // 2, width // 2),
        [like(rows // 2, width // 2)] * 4,
        [pltpu.VMEM((depth, width), BF16)],
        scalars=1,
    )(place, weight, weight, own, near, far, end)


def near_kernel(place_ref, weight_ref, near_ref, value_ref):
    value_ref[...] = jnp.dot(weight_ref[...], near_ref[...], preferred_element_type=F32)


def near_product_of(place, weight, near):
    rows, depth = weight.shape
    width = near.shape[1]
    step = 256
    return call(
        near_kernel,
        (rows // step,),
        [
            pl.BlockSpec((step, depth // 2), lambda i, p: (i, p[0])),
            pl.BlockSpec((depth // 2, width), lambda i, p: (0, 0)),
        ],
        pl.BlockSpec((step, width), lambda i, p: (i, 0)),
        jax.ShapeDtypeStruct((rows, width), F32),
        scalars=1,
    )(place, weight, near)


def far_kernel(place_ref, weight_ref, far_ref, end_ref, value_ref, keep_0, keep_1, send_0, send_1, units_ref):
    @pl.when((pl.program_id(0) == 0) & (place_ref[1] == 1))
    def _():
        units_ref[...] = far_ref[...]

    @pl.when((pl.program_id(0) == 0) & (place_ref[1] == 0))
    def _():
        units_ref[...] = end_ref[...]

    out = jnp.dot(weight_ref[...], units_ref[...], preferred_element_type=F32) + value_ref[...]
    put_halves(out, (keep_0, keep_1), (send_0, send_1))


def far_product_of(place, weight, far, end, value):
    rows, depth = weight.shape
    width = far.shape[1]
    step = 256
    unit_spec = pl.BlockSpec((depth // 2, width), lambda i, p: (0, 0))
    return call(
        far_kernel,
        (rows // step,),
        [
            pl.BlockSpec((step, depth // 2), lambda i, p: (i, 1 - p[0])),
            unit_spec,
            unit_spec,
            pl.BlockSpec((step, width), lambda i, p: (i, 0)),
        ],
        halves_specs(step, rows // step // 2, width // 2),
        [like(rows // 2, width // 2)] * 4,
        [pltpu.VMEM((depth // 2, width), BF16)],
        scalars=1,
    )(place, weight, far, end, value)


def cut_kernel(*refs):
    for one_ref, other_ref, keep_ref, send_ref in zip(refs[0:2], refs[2:4], refs[4:6], refs[6:8]):
        total = (one_ref[...].astype(F32) + other_ref[...].astype(F32)).astype(BF16)
        cut = keep_ref.shape[1]
        keep_ref[...] = total[:, :cut]
        send_ref[...] = total[:, cut:]


def cut_sums(ones, others):
    rows, width = ones[0].shape
    spec = pl.BlockSpec((rows, width), lambda i: (0, 0))
    half = pl.BlockSpec((rows, width // 2), lambda i: (0, 0))
    return call(cut_kernel, (1,), [spec] * 4, [half] * 4, [like(rows, width // 2)] * 4)(
        *ones, *others
    )


def finish_kernel(one_ref, two_ref, bias_ref, out_ref):
    total = one_ref[...].astype(F32) + two_ref[...].astype(F32)
    out_ref[...] = (total + bias_ref[...]).astype(BF16)


def finish(one, two, bias):
    rows, width = one.shape
    spec = pl.BlockSpec((rows, width), lambda i: (0, 0))
    bias_spec = pl.BlockSpec((rows, 1), lambda i: (0, 0))
    return call(finish_kernel, (1,), [spec, spec, bias_spec], spec, like(rows, width))(
        one, two, bias
    )


def shards(
    patches,
    ln_gain,
    ln_bias,
    first_weight,
    first_bias,
    second_weight,
    second_bias,
    text_embeds,
    vis_pos,
):
    wide = lax.axis_size("wide")
    narrow = lax.axis_size("narrow")
    wide_bits = wide.bit_length() - 1
    narrow_bits = narrow.bit_length() - 1
    line = wide // 2
    wide_at = lax.axis_index("wide")
    narrow_at = lax.axis_index("narrow")
    side_at = wide_at % 2
    line_at = wide_at // 2
    columns = patches.shape[0]
    hidden = first_weight.shape[2]
    features = second_weight.shape[0]
    tiles = patches.shape[1] // (4 * TILE_ROWS)
    prompt_rows = text_embeds.shape[1]
    depth = 4 * columns
    block = hidden // line

    merged, stats = merge(patches)
    other_bias = swap(second_bias, "wide", 1)
    stats = stats + swap(stats, "wide", 1)
    cuts = [0, features * 5 // 12 // 16 * 16]
    gain = ln_gain.astype(F32).T
    shift = ln_bias.astype(F32).T
    second_early = [second_weight[a:b] for a, b in zip(cuts, cuts[1:])]
    stats, second_early, other_bias, gain, shift = lax.optimization_barrier(
        (stats, second_early, other_bias, gain, shift)
    )
    for bit in range(1, wide_bits):
        stats = stats + swap(stats, "wide", 1 << bit)
    entries = 4.0 * D
    row_mean = stats[0] / entries
    row_var = stats[1] / entries - row_mean * row_mean
    inverse = lax.rsqrt(row_var + 1e-05)
    def normed(halves):
        return norm(merged, row_mean[None, :], inverse[None, :], gain, shift, halves)

    if line == 4:
        starts = [(line_at // 2 ^ i) * (hidden // 2) for i in range(2)]
    else:
        starts = [(line_at ^ i) * (hidden // line) for i in bit_reversed(wide_bits - 1)]
    block = hidden // len(starts)
    flat = first_weight.reshape(depth, hidden)
    own_bias = lax.dynamic_slice_in_dim(first_bias, starts[0], block, 0).astype(F32)[:, None]
    out_bias = [bias.astype(F32)[:, None] for bias in (second_bias, other_bias)]

    text_rows = narrow * prompt_rows - vis_pos.shape[0]
    first_row = narrow_at * prompt_rows
    grid = jnp.arange(prompt_rows, dtype=jnp.int32)[None, :]
    moves = {tile: [] for tile in range(tiles)}
    for tile in range(tiles):
        for step in range(1 - narrow, narrow):
            pairs = []
            for source in range(narrow):
                target = source + step
                low = (source * tiles + tile) * TILE_ROWS
                if (
                    0 <= target < narrow
                    and low < (target + 1) * prompt_rows
                    and low + text_rows + TILE_ROWS > target * prompt_rows
                ):
                    pairs.append((source, target))
            if pairs:
                moves[tile].append((step, pairs))
    groups = [(t,) for t in range(tiles)]

    def spot_of(step, tile, half):
        whose = narrow_at - step
        at = (jnp.clip(whose, 0, narrow - 1) * tiles + tile) * TILE_ROWS + half * HALF
        spot = lax.dynamic_slice_in_dim(vis_pos, at, HALF, 0) - first_row
        return jnp.where((whose >= 0) & (whose < narrow), spot, -1)

    hits = {}
    marked = jnp.zeros((prompt_rows,), bool)
    for group in groups:
        steps = sorted({step for tile in group for step, _ in moves[tile]})
        spots = [
            spot_of(step, tile, half)
            for step in steps
            for half in (side_at, 1 - side_at)
            for tile in group
        ]
        found = jnp.concatenate(spots)[:, None] == grid
        marked |= jnp.any(found, axis=0)
        hits[group] = found.astype(BF16)

    tile_order = bit_reversed(narrow_bits)
    outward = [(x, 2 + x) for x in (0, 1)] + [(6 + x, 4 + x) for x in (0, 1)]
    inward = [(b, a) for a, b in outward]
    middle = [(2 + x, 4 + x) for x in (0, 1)] + [(4 + x, 2 + x) for x in (0, 1)]
    is_middle = (line_at == 1) | (line_at == 2)
    place_at = jnp.stack([line_at // 2 % 2, is_middle.astype(jnp.int32)]).astype(jnp.int32)
    have, joined = {}, set()

    def put(key, value, flying=False):
        have[key] = value
        joined.discard(key)
        if not flying:
            joined.add(key)

    def fly(key, value, axis, pairs):
        if isinstance(pairs, int):
            pairs = [(i, i ^ pairs) for i in range(lax.axis_size(axis))]
        put(key, lax.ppermute(value, axis, pairs), True)
        put(("sent", key), value)

    def sync(needs):
        joined.update(needs)
        keys = [k for k in have if k in joined]
        have.update(zip(keys, lax.optimization_barrier([have[k] for k in keys])))
        for key in keys:
            if key[0] == "sent":
                del have[key]

    def hops(key, tile, stage):
        if stage == "high":
            return [(key, 0, narrow // 2, tile)]
        base = 0 if stage == "own" else narrow // 2
        found, result = [base], []
        for bit in reversed(range(narrow_bits - 1)):
            result += [(key, d, d + (1 << bit), tile) for d in found]
            found += [d + (1 << bit) for d in found]
        return result

    row_parts = 2 if columns % 16 == 0 else 1

    def of(key, tile, stage):
        return [
            (key, to, tile, part)
            for key, _, to, tile in hops(key, tile, stage)
            for part in range(row_parts)
        ]

    def norm_step(key, tile):
        theirs, mine = 2 * tile + 1 - side_at, 2 * tile + side_at
        halves = {"theirs": [theirs], "mine": [mine], "both": [theirs, mine]}[key]
        for part, value in enumerate(normed(halves)):
            put((key, 0, tile, part), value)

    def gather_step(key, tile, stage):
        for key, origin, to, tile in hops(key, tile, stage):
            for part in range(row_parts):
                fly((key, to, tile, part), have[key, origin, tile, part], "narrow", origin ^ to)

    def pieces_of(key, tile):
        return [[have[key, d, tile, part] for part in range(row_parts)] for d in tile_order]

    def drop(tile):
        for key in [key for key in have if len(key) == 4 and key[2] == tile]:
            del have[key]

    def send_theirs(tile, part):
        key = "both" if tile else "theirs"
        pieces = pieces_of(key, tile)
        if part == "all":
            sent = product(have["first",], pieces, 0, 0, hidden)
        else:
            sent = product(have["first",], pieces, 0, 0 if part == "near" else block, block)
        put(("theirs", part, tile), sent)

    def fly_theirs(tile, part):
        if tile < tiles:
            fly(("came", part, tile), have.pop(("theirs", part, tile)), "wide", 1)

    def send_and_keep(tile):
        if line == 4:
            near, far, own = products(have["first",], pieces_of("both", tile))
            put(("theirs", "near", tile), near)
            put(("theirs", "far", tile), far)
            put(("own", tile), own)
            drop(tile)
        else:
            send_theirs(tile, "all")
            fly_theirs(tile, "all")
            keep_mine(tile)

    def keep_mine(tile):
        key = "both" if tile else "mine"
        own = product(have["first",], pieces_of(key, tile), 1 if tile else 0, 0, hidden)
        put(("own", tile), own)
        drop(tile)

    def second_columns(at):
        return lax.dynamic_slice_in_dim(have["second",], at, block, 1)

    def join_second():
        parts = [second_weight] + [have.pop(("second", i)) for i in range(2)]
        put(("second",), jnp.concatenate(parts, axis=0))

    def far_ready(tile):
        if tile:
            fly_theirs(tile, "near")
        put(("far", tile), add(have["own", tile], have.pop(("came", "far", tile)), block))

    def near_ready(tile):
        fly_theirs(tile + 1, "far")
        put(("near", tile), add(have.pop(("own", tile)), have.pop(("came", "near", tile))))

    def far_out(tile):
        if tile < tiles:
            fly(("far_came", tile), have["far", tile], "wide", outward)

    def near_out(tile):
        fly(("near_came", tile), have["near", tile], "wide", outward)

    def across(tile):
        far = add(have.pop(("far", tile)), have.pop(("far_came", tile)))
        fly(("across", tile), far, "wide", middle)

    def activate(tile):
        terms = [have.pop((key, tile)) for key in ("near", "near_came", "across")]
        act = activated_sum(*terms, own_bias)
        put(("act", tile), act)
        fly(("far_act", tile), act, "wide", middle)
        fly(("near_act", tile), act, "wide", inward)

    def far_in(tile):
        fly(("far_act_end", tile), have["far_act", tile], "wide", inward)

    def near_product(tile):
        near = jnp.where(is_middle, have["act", tile], have["near_act", tile])
        put(("near_value", tile), near_product_of(place_at, have["second",], near))

    def second_product(group):
        tile = group[0]
        if line == 4 and tile == tiles - 1:
            far, end = have.pop(("far_act", tile)), have.pop(("far_act_end", tile))
            value = have.pop(("near_value", tile))
            out = far_product_of(place_at, have["second",], far, end, value)
            del have["act", tile], have["near_act", tile]
        elif line == 4:
            names = ("act", "near_act", "far_act", "far_act_end")
            terms = [have.pop((name, tile)) for name in names]
            out = second_product_of(place_at, have["second",], *terms)
        else:
            units = jnp.concatenate(have.pop(("acts", tile)), axis=0)
            second = jnp.concatenate([second_columns(s) for s in starts], axis=1)
            value = jnp.dot(second, units, preferred_element_type=F32).astype(BF16)
            cut = value.shape[1] // 2
            value = [value[:features], value[features:]]
            out = [v[:, :cut] for v in value] + [v[:, cut:] for v in value]
        for i in (1, 0):
            put(("value", i, group), out[i])
            fly(("part", i, group), out[2 + i], "narrow", 1)

    def halve(bit):
        def step(tile):
            if bit == 1:
                came = have.pop(("came", "all", tile))
                total = have.pop(("own", tile)).astype(F32) + came.astype(F32)
            else:
                total = have.pop(("sum", tile)).astype(F32) + have.pop(("part", tile)).astype(F32)
            total = total.astype(BF16)
            cut = total.shape[0] // 2
            put(("sum", tile), total[:cut])
            put(("part", tile), swap(total[cut:], "wide", 1 << bit))

        return step

    def double(bit):
        def step(tile):
            if bit == wide_bits - 1:
                total = have.pop(("sum", tile)).astype(F32) + have.pop(("part", tile)).astype(F32)
                act = jax.nn.gelu(total + own_bias, approximate=False).astype(BF16)
                put(("acts", tile), [act])
            acts = have["acts", tile]
            put(("acts", tile), acts + [swap(act, "wide", 1 << bit) for act in acts])

        return step

    def narrow_step(group, bit):
        values = [have["value", i, group] for i in range(2)]
        out = cut_sums(values, [have["part", i, group] for i in range(2)])
        for i in (1, 0):
            put(("value", i, group), out[i])
            fly(("part", i, group), out[2 + i], "narrow", 1 << bit)

    def finished(group, i):
        return finish(have.pop(("value", i, group)), have.pop(("part", i, group)), out_bias[i])

    def trade(group):
        fly(("traded", group), finished(group, 1), "wide", 1)

    def keep(group):
        put(("kept", group), finished(group, 0))

    def steps_of(group):
        pairs = {}
        for tile in group:
            for step, some in moves[tile]:
                pairs[step] = sorted(set(pairs.get(step, []) + some))
        return dict(sorted(pairs.items()))

    def halo(group):
        whole = jnp.concatenate([have.pop(("kept", group)), have.pop(("traded", group))], axis=1)
        for step, pairs in steps_of(group).items():
            if step:
                fly(("moved", step, group), whole, "narrow", pairs)
            else:
                put(("moved", step, group), whole)

    def place(group):
        keys = [("moved", step, group) for step in steps_of(group)]
        moved = jnp.concatenate([have.pop(key) for key in keys], axis=1)
        more = jnp.dot(moved, hits[group], preferred_element_type=F32)
        put(("placed",), have["placed",] + more.astype(BF16))

    def late_second():
        fly(("second", 1), have.pop(("second_late",))[cuts[-1] :], "wide", 1)

    def order_first():
        if line == 4:
            put(("first",), turn(have["first",], place_at[:1]))
        else:
            cut = [lax.dynamic_slice_in_dim(have["first",], s, block, 1) for s in starts]
            put(("first",), jnp.concatenate(cut, axis=1).T)

    def clear_marked():
        put(("placed",), jnp.where(marked[None, :], jnp.zeros((), BF16), have["placed",]))

    put(("first",), flat)
    put(("placed",), text_embeds)
    put(("second_late",), second_weight)
    for i, piece in enumerate(second_early):
        fly(("second", i), piece, "wide", 1)

    events = []

    def at(time, needs, step, *args):
        events.append((time, len(events), needs, step, args))

    parts = ["far", "near"] if line == 4 else ["all"]
    nothing = lambda: None
    at(19, [], norm_step, "theirs", 0)
    at(20, [], gather_step, "theirs", 0, "high")
    at(20.1, [], gather_step, "theirs", 0, "own")
    at(21, [], norm_step, "mine", 0)
    at(22, [], order_first)
    at(30, of("theirs", 0, "high"), gather_step, "theirs", 0, "rest")
    at(31, [], gather_step, "mine", 0, "high")
    at(31.1, [], norm_step, "both", 1)
    at(31.2, [], gather_step, "both", 1, "high")
    needs = of("theirs", 0, "own") + of("theirs", 0, "rest") + [("second", 0)]
    at(34, needs, send_theirs, 0, parts[0])
    at(34.1, [], fly_theirs, 0, parts[0])
    at(42, of("mine", 0, "high"), gather_step, "mine", 0, "own")
    at(42.1, [], gather_step, "mine", 0, "rest")
    if line == 4:
        at(42.2, [], send_theirs, 0, "near")
        at(42.3, [], fly_theirs, 0, "near")
    at(45, of("mine", 0, "own") + of("mine", 0, "rest"), keep_mine, 0)
    for tile in range(2, tiles):
        at(45.1 + 0.1 * tile, [], norm_step, "both", tile)
    at(45.6, [], gather_step, "both", 1, "own")
    at(47.5, [], clear_marked)
    tick = 19.5
    for tile in range(1, tiles):
        arrived = 65 + tick * (tile - 1) + 1
        at(arrived, of("both", tile, "high"), gather_step, "both", tile, "rest")
        if tile + 1 < tiles:
            at(arrived + 0.1, [], gather_step, "both", tile + 1, "high")
            at(arrived + 0.2, [], gather_step, "both", tile + 1, "own")
        at(arrived + 3, of("both", tile, "own") + of("both", tile, "rest"), nothing)
        at(70 if tile == 1 else 65 + tick * (2 * tile - 2) + 5, [], send_and_keep, tile)
    last = 65 + tick * (2 * tiles - 1)
    at(last + 0.2, [], late_second)
    for tile in range(tiles):
        if line == 4:
            a = 65 + tick * (2 * tile + 1)
            b = a + tick
            if tile == 0:
                at(a - tick, [("came", "far", 0)], far_ready, 0)
                at(a - tick, [], far_out, 0)
            at(a, [("came", "near", tile)], near_ready, tile)
            at(a + 0.1, [("far_came", tile)], near_out, tile)
            at(a + 0.1, [], across, tile)
            if tile + 1 < tiles:
                at(b, [("came", "far", tile + 1)], far_ready, tile + 1)
            at(b + 0.1, [("near_came", tile)], far_out, tile + 1)
            at(b + 0.2, [("across", tile)], activate, tile)
            at(b + tick + 0.3, [("far_act", tile), ("near_act", tile)], far_in, tile)
            at(b + 2 * tick + 0.3, [("far_act_end", tile)], nothing)
        else:
            base = 74 + 37 * tile
            for i, bit in enumerate(range(1, wide_bits)):
                needs = [("part", tile)] if i else [("came", "all", tile)]
                at(base + 8 * i, needs, halve(bit), tile)
            for i, bit in enumerate(reversed(range(1, wide_bits))):
                needs = [] if i else [("part", tile)]
                at(base + 35 + 8 * i, needs, double(bit), tile)
    done = last + 3 * tick + 0.4
    at(done - tick - 9, [("second", 1)], join_second)
    if line == 4:
        at(done - 3, [], near_product, tiles - 1)
    for i, group in enumerate(groups):
        if line == 4 and tiles == 4:
            times = (
                (-28, -18, -6, 6, 10),
                (-17, -7, 7, 12, 16),
                (-16, -6.9, 13, 18, 23),
                (0, 4, 12, 19, 24),
            )[i]
        else:
            times = (10 * i, 10 * i + 1, 10 * i + 5, 10 * i + 6, 10 * i + 7)
        times = [done + time for time in times]
        at(times[0], [], second_product, group)
        for bit in range(1, narrow_bits):
            needs = [("part", 0, group), ("part", 1, group)]
            at(times[1] + 0.1 * bit, needs, narrow_step, group, bit)
        at(times[2], [("part", 1, group)], trade, group)
        at(times[2] + 0.1, [("part", 0, group)], keep, group)
        at(times[3], [("traded", group)], halo, group)
        flown = [("moved", step, group) for step in steps_of(group) if step]
        at(times[4], flown, place, group)
    for _, _, needs, step, args in sorted(events, key=lambda e: e[:2]):
        sync(needs)
        step(*args)
    return have["placed",]


def solution(mesh):
    in_specs = (
        P("wide", "narrow"),
        P(None, "wide"),
        P(None, "wide"),
        P(None, "wide", "narrow"),
        P("narrow"),
        P("wide", "narrow"),
        P("wide"),
        P("wide", "narrow"),
        P(),
    )
    out_specs = P("wide", "narrow")
    return jax.shard_map(shards, mesh=mesh, in_specs=in_specs, out_specs=out_specs, check_vma=False)
```

```python
import functools

import jax
import jax.numpy as jnp
from jax import lax
from jax.experimental import pallas as pl
from jax.experimental.pallas import tpu as pltpu
from jax.sharding import PartitionSpec as P

D = 3200
TILE_SIDE = 32
TILE_ROWS = 256
HALF = 128
COLS = 512
PAD = 16
F32 = jnp.float32
BF16 = jnp.bfloat16
WIDE, NARROW = "wide", "narrow"
(
    SENT,
    HIGH,
    OWN,
    THEIRS,
    MINE,
    BOTH,
    ALL,
    FIRST,
    NEAR,
    CAME,
    FAR,
    SECOND,
    FAR_CAME,
    NEAR_CAME,
    ACROSS,
    ACT,
    FAR_ACT,
    NEAR_ACT,
    FAR_ACT_END,
    NEAR_VALUE,
    ACTS,
    VALUE,
    PART,
    SUM,
    TRADED,
    KEPT,
    MOVED,
    PLACED,
    REST,
    HITS,
    POS,
) = range(31)


def bit_reversed(bits):
    return [sum(((p >> b) & 1) << (bits - 1 - b) for b in range(bits)) for p in range(1 << bits)]


def swap(value, axis, mask):
    count = lax.axis_size(axis)
    return lax.ppermute(value, axis, [(i, i ^ mask) for i in range(count)])


def merge_kernel(patch_ref, order_ref, *refs):
    merged_refs, stats_ref = refs[:-1], refs[-1]
    mixed = jnp.dot(patch_ref[...], order_ref[...], preferred_element_type=F32)
    total = jnp.zeros((1, HALF), F32)
    squares = jnp.zeros((1, HALF), F32)
    for slot in range(4):
        part = mixed[:, slot * HALF : (slot + 1) * HALF]
        total += jnp.sum(part, axis=0, keepdims=True)
        squares += jnp.sum(part * part, axis=0, keepdims=True)
    stats_ref[0:1, :] = total
    stats_ref[1:2, :] = squares
    for tile, merged_ref in enumerate(merged_refs):

        @pl.when(pl.program_id(0) // 2 == tile)
        def _():
            for slot in range(4):
                merged_ref[0, slot] = mixed[:, slot * HALF : (slot + 1) * HALF].astype(BF16)


def merge(patches):
    columns, width = patches.shape
    steps = width // COLS
    side = TILE_SIDE // 2
    source = lax.broadcasted_iota(jnp.int32, (COLS, COLS), 0)
    target = lax.broadcasted_iota(jnp.int32, (COLS, COLS), 1)
    slot = target // HALF
    row = target % HALF
    wanted = (
        (row // side) * (4 * side) + (slot // 2) * (2 * side) + (row % side) * 2 + slot % 2
    )
    order = (source == wanted).astype(BF16)

    def tile_spec(tile):
        return pl.BlockSpec(
            (1, 4, columns, HALF), lambda i: (jnp.clip(i - 2 * tile, 0, 1), 0, 0, 0)
        )

    tiles = steps // 2
    out = pl.pallas_call(
        merge_kernel,
        grid=(steps,),
        in_specs=[
            pl.BlockSpec((columns, COLS), lambda i: (0, i)),
            pl.BlockSpec((COLS, COLS), lambda i: (0, 0)),
        ],
        out_specs=[tile_spec(tile) for tile in range(tiles)]
        + [pl.BlockSpec((2, HALF), lambda i: (0, i))],
        out_shape=[jax.ShapeDtypeStruct((2, 4, columns, HALF), BF16)] * tiles
        + [jax.ShapeDtypeStruct((2, steps * HALF), F32)],
        compiler_params=pltpu.CompilerParams(vmem_limit_bytes=16 * 1024 * 1024),
    )(patches, order)
    return out[:-1], out[-1]


def call(kernel, grid, in_specs, out_specs, out_shape, scratch_shapes=(), scalars=0, flops=1):
    return pl.pallas_call(
        kernel,
        grid_spec=pltpu.PrefetchScalarGridSpec(
            num_scalar_prefetch=scalars,
            grid=grid,
            in_specs=in_specs,
            out_specs=out_specs,
            scratch_shapes=scratch_shapes,
        ),
        out_shape=out_shape,
        cost_estimate=pl.CostEstimate(flops=flops, bytes_accessed=1, transcendentals=0),
        compiler_params=pltpu.CompilerParams(vmem_limit_bytes=16 * 1024 * 1024),
    )


def like(rows, width):
    return jax.ShapeDtypeStruct((rows, width), BF16)


def norm_kernel(half_ref, merged_ref, mean_ref, scale_ref, gain_ref, shift_ref, out_ref):
    for slot in range(4):
        values = merged_ref[0, slot].astype(F32)
        gain, shift = gain_ref[:, slot : slot + 1], shift_ref[:, slot : slot + 1]
        result = (values - mean_ref[...]) * scale_ref[...] * gain + shift
        out_ref[slot] = result.astype(BF16)


def norm(merged, mean, scale, gain, shift, tile, halves):
    columns = merged.shape[2]
    out = call(
        norm_kernel,
        (len(halves),),
        [
            pl.BlockSpec((1, 4, columns, HALF), lambda i, h: (h[i], 0, 0, 0)),
            pl.BlockSpec((1, HALF), lambda i, h: (0, h[i] + 2 * tile)),
            pl.BlockSpec((1, HALF), lambda i, h: (0, h[i] + 2 * tile)),
            pl.BlockSpec((columns, 4), lambda i, h: (0, 0)),
            pl.BlockSpec((columns, 4), lambda i, h: (0, 0)),
        ],
        pl.BlockSpec((4, columns, HALF), lambda i, h: (0, 0, i)),
        jax.ShapeDtypeStruct((4, columns, len(halves) * HALF), BF16),
        scalars=1,
    )(jnp.stack(halves).astype(jnp.int32), merged, mean, scale, gain, shift)
    return [out.reshape(-1, len(halves) * HALF)]


def turn_kernel(first_ref, flat_ref, out_ref):
    out_ref[...] = flat_ref[...].T


def turn(flat, near):
    depth, hidden = flat.shape
    step = 256
    half = hidden // 2 // step
    return call(
        turn_kernel,
        (2 * half,),
        [pl.BlockSpec((depth, step), lambda i, n: (0, (i // half + n[0]) % 2 * half + i % half))],
        pl.BlockSpec((step, depth), lambda i, n: (i, 0)),
        like(hidden, depth),
        scalars=1,
    )(near, flat)


def stage(rows_ref, tile_refs, columns, places):
    for parts, place in zip(tile_refs, places):
        row = 0
        for part in parts:
            rows_ref[row : row + part.shape[0], place : place + HALF] = part[:, columns]
            row += part.shape[0]


def by_tile(refs, count):
    return [refs[i : i + count] for i in range(0, len(refs), count)]


def product_kernel(count, weight_ref, *refs):
    tile_refs, out_ref, rows_ref = by_tile(refs[:-2], count), refs[-2], refs[-1]

    @pl.when(pl.program_id(0) == 0)
    def _():
        places = [i * HALF for i in range(len(tile_refs))]
        stage(rows_ref, tile_refs, slice(None), places)

    out = jnp.dot(weight_ref[...], rows_ref[...], preferred_element_type=F32)
    out_ref[...] = out.astype(out_ref.dtype)


def product(weight, tiles, half, start, rows):
    depth = weight.shape[1]
    step = 256 if rows % 256 == 0 else rows
    width = len(tiles) * HALF
    parts = [part for tile in tiles for part in tile]
    return call(
        functools.partial(product_kernel, len(tiles[0])),
        (rows // step,),
        [pl.BlockSpec((step, depth), lambda i: (i + start // step, 0))]
        + [pl.BlockSpec((part.shape[0], HALF), lambda i: (0, half)) for part in parts],
        pl.BlockSpec((step, width), lambda i: (i, 0)),
        like(rows, width),
        [pltpu.VMEM((depth, width), BF16)],
    )(weight, *parts)


def products_kernel(count, weight_ref, *refs):
    tile_refs, (near_ref, far_ref, own_ref, rows_ref) = by_tile(refs[:-4], count), refs[-4:]
    width = len(tile_refs) * HALF
    step = pl.program_id(0)
    half = pl.num_programs(0) // 2

    @pl.when(step == 0)
    def _():
        places = [i * HALF for i in range(len(tile_refs))]
        stage(rows_ref, tile_refs, slice(0, HALF), places)
        stage(rows_ref, tile_refs, slice(HALF, 2 * HALF), [width + place for place in places])

    out = jnp.dot(weight_ref[...], rows_ref[...], preferred_element_type=F32).astype(BF16)
    own_ref[...] = out[:, width:]

    @pl.when(step < half)
    def _():
        near_ref[...] = out[:, :width]

    @pl.when(step >= half)
    def _():
        far_ref[...] = out[:, :width]


def products(weight, tiles):
    rows, depth = weight.shape
    step = 256
    half = rows // step // 2
    width = len(tiles) * HALF
    parts = [part for tile in tiles for part in tile]
    return call(
        functools.partial(products_kernel, len(tiles[0])),
        (2 * half,),
        [pl.BlockSpec((step, depth), lambda i: (i, 0))]
        + [pl.BlockSpec((part.shape[0], 2 * HALF), lambda i: (0, 0)) for part in parts],
        [
            pl.BlockSpec((step, width), lambda i: (jnp.minimum(i, half - 1), 0)),
            pl.BlockSpec((step, width), lambda i: (jnp.maximum(i - half, 0), 0)),
            pl.BlockSpec((step, width), lambda i: (i, 0)),
        ],
        [like(rows // 2, width), like(rows // 2, width), like(rows, width)],
        [pltpu.VMEM((depth, 2 * width), BF16)],
    )(weight, *parts)


def add_kernel(one_ref, other_ref, out_ref):
    out_ref[...] = (one_ref[...].astype(F32) + other_ref[...].astype(F32)).astype(BF16)


def add(one, other, start=0):
    rows, width = other.shape
    step = rows // 2
    spec = pl.BlockSpec((step, width), lambda i: (i, 0))
    one_spec = pl.BlockSpec((step, width), lambda i: (i + start // step, 0))
    return call(add_kernel, (2,), [one_spec, spec], spec, like(rows, width))(one, other)


def activate_kernel(one_ref, two_ref, three_ref, bias_ref, out_ref):
    rows = one_ref.shape[0]
    step = rows // 4
    for i in range(4):
        some = slice(i * step, (i + 1) * step)
        total = one_ref[some, :].astype(F32) + two_ref[some, :].astype(F32)
        total = total + three_ref[some, :].astype(F32) + bias_ref[some, :]
        out_ref[some, :] = (0.5 * total * (1.0 + lax.erf(total * 0.5**0.5))).astype(BF16)
    if out_ref.shape[0] > rows:
        out_ref[rows:, :] = jnp.zeros((out_ref.shape[0] - rows, out_ref.shape[1]), BF16)


def activated_sum(one, two, three, bias, pad):
    rows, width = one.shape
    spec = pl.BlockSpec((rows, width), lambda i: (0, 0))
    bias_spec = pl.BlockSpec((rows, 1), lambda i: (0, 0))
    out_spec = pl.BlockSpec((rows + pad, width), lambda i: (0, 0))
    return call(
        activate_kernel, (1,), [spec, spec, spec, bias_spec], out_spec, like(rows + pad, width)
    )(one, two, three, bias)


def weight_specs(step, half, depth, column):
    return [
        pl.BlockSpec((step, depth), lambda i, p: (jnp.minimum(i, half - 1), column(p))),
        pl.BlockSpec((step, depth), lambda i, p: (jnp.maximum(i - half, 0), column(p))),
    ]


def pick(refs):
    own = pl.program_id(0) < pl.num_programs(0) // 2
    return jnp.where(own, refs[0][...], refs[1][...])


def second_kernel(place_ref, *refs):
    weight_refs, (own_ref, near_ref, far_ref, end_ref, keep_ref, send_ref, units_ref) = refs[:4], refs[4:]
    half = weight_refs[0].shape[1]

    @pl.when((pl.program_id(0) == 0) & (place_ref[1] == 1))
    def _():
        units_ref[:half, :] = own_ref[:half, :]
        units_ref[half:, :] = far_ref[:half, :]

    @pl.when((pl.program_id(0) == 0) & (place_ref[1] == 0))
    def _():
        units_ref[:half, :] = near_ref[:half, :]
        units_ref[half:, :] = end_ref[:half, :]

    near, far = pick(weight_refs[:2]), pick(weight_refs[2:])
    out = jnp.dot(near, units_ref[:half, :], preferred_element_type=F32)
    out += jnp.dot(far, units_ref[half:, :], preferred_element_type=F32)
    cut = keep_ref.shape[1]
    keep_ref[...] = out[:, :cut].astype(BF16)
    send_ref[...] = out[:, cut:].astype(BF16)


def second_product_of(place, weights, own, near, far, end):
    rows, depth = weights[0].shape
    width = own.shape[1]
    step = 256
    half = rows // step
    unit_spec = pl.BlockSpec(own.shape, lambda i, p: (0, 0))
    spec = pl.BlockSpec((step, width // 2), lambda i, p: (i, 0))
    return call(
        second_kernel,
        (2 * half,),
        weight_specs(step, half, depth // 2, lambda p: p[0])
        + weight_specs(step, half, depth // 2, lambda p: 1 - p[0])
        + [unit_spec] * 4,
        [spec, spec],
        [like(2 * rows, width // 2)] * 2,
        [pltpu.VMEM((depth, width), BF16)],
        scalars=1,
    )(place, *weights, *weights, own, near, far, end)


def near_kernel(place_ref, own_weight_ref, other_weight_ref, own_ref, near_ref, value_ref, units_ref):
    half = own_weight_ref.shape[1]

    @pl.when((pl.program_id(0) == 0) & (place_ref[1] == 1))
    def _():
        units_ref[...] = own_ref[:half, :]

    @pl.when((pl.program_id(0) == 0) & (place_ref[1] == 0))
    def _():
        units_ref[...] = near_ref[:half, :]

    weight = pick((own_weight_ref, other_weight_ref))
    value_ref[...] = jnp.dot(weight, units_ref[...], preferred_element_type=F32)


def near_product_of(place, weights, own, near):
    rows, depth = weights[0].shape
    width = near.shape[1]
    step = 256
    half = rows // step
    unit_spec = pl.BlockSpec(near.shape, lambda i, p: (0, 0))
    return call(
        near_kernel,
        (2 * half,),
        weight_specs(step, half, depth // 2, lambda p: p[0]) + [unit_spec] * 2,
        pl.BlockSpec((step, width), lambda i, p: (i, 0)),
        jax.ShapeDtypeStruct((2 * rows, width), F32),
        [pltpu.VMEM((depth // 2, width), BF16)],
        scalars=1,
    )(place, *weights, own, near)


def far_kernel(place_ref, own_weight_ref, other_weight_ref, far_ref, end_ref, value_ref, keep_ref, send_ref, units_ref):
    half = own_weight_ref.shape[1]

    @pl.when((pl.program_id(0) == 0) & (place_ref[1] == 1))
    def _():
        units_ref[...] = far_ref[:half, :]

    @pl.when((pl.program_id(0) == 0) & (place_ref[1] == 0))
    def _():
        units_ref[...] = end_ref[:half, :]

    weight = pick((own_weight_ref, other_weight_ref))
    out = jnp.dot(weight, units_ref[...], preferred_element_type=F32) + value_ref[...]
    cut = keep_ref.shape[1]
    keep_ref[...] = out[:, :cut].astype(BF16)
    send_ref[...] = out[:, cut:].astype(BF16)


def far_product_of(place, weights, far, end, value):
    rows, depth = weights[0].shape
    width = far.shape[1]
    step = 256
    half = rows // step
    unit_spec = pl.BlockSpec(far.shape, lambda i, p: (0, 0))
    spec = pl.BlockSpec((step, width // 2), lambda i, p: (i, 0))
    return call(
        far_kernel,
        (2 * half,),
        weight_specs(step, half, depth // 2, lambda p: 1 - p[0])
        + [unit_spec, unit_spec, pl.BlockSpec((step, width), lambda i, p: (i, 0))],
        [spec, spec],
        [like(2 * rows, width // 2)] * 2,
        [pltpu.VMEM((depth // 2, width), BF16)],
        scalars=1,
    )(place, *weights, far, end, value)


def cut_kernel(one_ref, other_ref, keep_ref, send_ref):
    total = (one_ref[...].astype(F32) + other_ref[...].astype(F32)).astype(BF16)
    cut = keep_ref.shape[1]
    keep_ref[...] = total[:, :cut]
    send_ref[...] = total[:, cut:]


def cut_sum(one, other):
    rows, width = one.shape
    spec = pl.BlockSpec((rows // 2, width), lambda i: (i, 0))
    half = pl.BlockSpec((rows // 2, width // 2), lambda i: (i, 0))
    return call(cut_kernel, (2,), [spec, spec], [half, half], [like(rows, width // 2)] * 2)(
        one, other
    )


def finish_kernel(one_ref, two_ref, bias_ref, out_ref):
    total = one_ref[...].astype(F32) + two_ref[...].astype(F32)
    out_ref[...] = (total + bias_ref[...]).astype(BF16)


def finish(one, two, bias, half):
    rows, width = bias.shape[0], one.shape[1]
    spec = pl.BlockSpec((rows, width), lambda i: (half, 0))
    out_spec = pl.BlockSpec((rows, width), lambda i: (0, 0))
    bias_spec = pl.BlockSpec((rows, 1), lambda i: (0, 0))
    return call(finish_kernel, (1,), [spec, spec, bias_spec], out_spec, like(rows, width))(
        one, two, bias
    )


def shards(
    patches,
    ln_gain,
    ln_bias,
    first_weight,
    first_bias,
    second_weight,
    second_bias,
    text_embeds,
    vis_pos,
):
    wide = lax.axis_size(WIDE)
    narrow = lax.axis_size(NARROW)
    wide_bits = wide.bit_length() - 1
    narrow_bits = narrow.bit_length() - 1
    line = wide // 2
    wide_at = lax.axis_index(WIDE)
    narrow_at = lax.axis_index(NARROW)
    side_at = wide_at % 2
    line_at = wide_at // 2
    columns = patches.shape[0]
    hidden = first_weight.shape[2]
    features = second_weight.shape[0]
    tiles = patches.shape[1] // (4 * TILE_ROWS)
    prompt_rows = text_embeds.shape[1]
    depth = 4 * columns
    block = hidden // line

    merged, stats = merge(patches)
    other_bias = swap(second_bias, WIDE, 1)
    stats = stats + swap(stats, WIDE, 1)
    early = features // 2 // 16 * 16
    gain = ln_gain.astype(F32).T
    shift = ln_bias.astype(F32).T
    second_early = second_weight[:early]
    stats, second_early, other_bias, gain, shift = lax.optimization_barrier(
        (stats, second_early, other_bias, gain, shift)
    )
    for bit in range(1, wide_bits):
        stats = stats + swap(stats, WIDE, 1 << bit)
    entries = 4.0 * D
    row_mean = stats[0] / entries
    row_var = stats[1] / entries - row_mean * row_mean
    inverse = lax.rsqrt(row_var + 1e-05)
    def normed(tile, halves):
        return norm(merged[tile], row_mean[None, :], inverse[None, :], gain, shift, tile, halves)

    if line == 4:
        starts = [(line_at // 2 ^ i) * (hidden // 2) for i in range(2)]
    else:
        starts = [(line_at ^ i) * (hidden // line) for i in bit_reversed(wide_bits - 1)]
    block = hidden // len(starts)
    flat = first_weight.reshape(depth, hidden)
    own_bias = lax.dynamic_slice_in_dim(first_bias, starts[0], block, 0).astype(F32)[:, None]
    out_bias = [bias.astype(F32)[:, None] for bias in (second_bias, other_bias)]

    text_rows = narrow * prompt_rows - vis_pos.shape[0]
    first_row = narrow_at * prompt_rows
    grid = jnp.arange(prompt_rows, dtype=jnp.int32)[None, :]
    moves = {tile: [] for tile in range(tiles)}
    for tile in range(tiles):
        for step in range(1 - narrow, narrow):
            pairs = []
            for source in range(narrow):
                target = source + step
                low = (source * tiles + tile) * TILE_ROWS
                if (
                    0 <= target < narrow
                    and low < (target + 1) * prompt_rows
                    and low + text_rows + TILE_ROWS > target * prompt_rows
                ):
                    pairs.append((source, target))
            if pairs:
                moves[tile].append((step, pairs))
    groups = [(t,) for t in range(tiles)]

    tile_order = bit_reversed(narrow_bits)
    outward = [(x, 2 + x) for x in (0, 1)] + [(6 + x, 4 + x) for x in (0, 1)]
    inward = [(b, a) for a, b in outward]
    middle = [(2 + x, 4 + x) for x in (0, 1)] + [(4 + x, 2 + x) for x in (0, 1)]
    is_middle = (line_at == 1) | (line_at == 2)
    place_at = jnp.stack([line_at // 2 % 2, is_middle.astype(jnp.int32)]).astype(jnp.int32)
    have, joined = {}, set()

    def put(key, value, flying=False):
        have[key] = value
        joined.discard(key)
        if not flying:
            joined.add(key)

    def fly(key, value, axis, pairs):
        if isinstance(pairs, int):
            pairs = [(i, i ^ pairs) for i in range(lax.axis_size(axis))]
        put(key, lax.ppermute(value, axis, pairs), True)
        put((SENT, key), value)

    def sync(needs):
        joined.update(needs)
        keys = [k for k in have if k in joined]
        have.update(zip(keys, lax.optimization_barrier([have[k] for k in keys])))
        for key in keys:
            if key[0] == SENT:
                del have[key]

    def hops(key, tile, stage):
        if stage == HIGH:
            return [(key, 0, narrow // 2, tile)]
        base = 0 if stage == OWN else narrow // 2
        found, result = [base], []
        for bit in reversed(range(narrow_bits - 1)):
            result += [(key, d, d + (1 << bit), tile) for d in found]
            found += [d + (1 << bit) for d in found]
        return result

    row_parts = 1

    def of(key, tile, stage):
        return [
            (key, to, tile, part)
            for key, _, to, tile in hops(key, tile, stage)
            for part in range(row_parts)
        ]

    def norm_step(key, tile):
        theirs, mine = 1 - side_at, side_at
        halves = {THEIRS: [theirs], MINE: [mine], BOTH: [theirs, mine]}[key]
        for part, value in enumerate(normed(tile, halves)):
            put((key, 0, tile, part), value)

    def gather_step(key, tile, stage):
        for key, origin, to, tile in hops(key, tile, stage):
            for part in range(row_parts):
                fly((key, to, tile, part), have[key, origin, tile, part], NARROW, origin ^ to)

    def pieces_of(key, tile):
        return [[have[key, d, tile, part] for part in range(row_parts)] for d in tile_order]

    def drop(tile):
        for key in [key for key in have if len(key) == 4 and key[2] == tile]:
            del have[key]

    def send_theirs(tile, part):
        key = BOTH if tile else THEIRS
        pieces = pieces_of(key, tile)
        if part == ALL:
            sent = product(have[FIRST,], pieces, 0, 0, hidden)
        else:
            sent = product(have[FIRST,], pieces, 0, 0 if part == NEAR else block, block)
        put((THEIRS, part, tile), sent)

    def fly_theirs(tile, part):
        if tile < tiles:
            fly((CAME, part, tile), have.pop((THEIRS, part, tile)), WIDE, 1)

    def send_and_keep(tile):
        if line == 4:
            near, far, own = products(have[FIRST,], pieces_of(BOTH, tile))
            put((THEIRS, NEAR, tile), near)
            put((THEIRS, FAR, tile), far)
            put((OWN, tile), own)
            drop(tile)
        else:
            send_theirs(tile, ALL)
            fly_theirs(tile, ALL)
            keep_mine(tile)

    def keep_mine(tile):
        key = BOTH if tile else MINE
        own = product(have[FIRST,], pieces_of(key, tile), 1 if tile else 0, 0, hidden)
        put((OWN, tile), own)
        drop(tile)

    def second_weights():
        return [second_weight, have[SECOND,]]

    def second_columns(at):
        parts = [lax.dynamic_slice_in_dim(part, at, block, 1) for part in second_weights()]
        return jnp.concatenate(parts, axis=0)

    def join_second():
        parts = [have.pop((SECOND, 0)), have.pop((SECOND, 1))]
        put((SECOND,), jnp.concatenate(parts, axis=0))

    def far_ready(tile):
        if tile:
            fly_theirs(tile, NEAR)
        put((FAR, tile), add(have[OWN, tile], have.pop((CAME, FAR, tile)), block))

    def near_ready(tile):
        fly_theirs(tile + 1, FAR)
        put((NEAR, tile), add(have.pop((OWN, tile)), have.pop((CAME, NEAR, tile))))

    def far_out(tile):
        if tile < tiles:
            fly((FAR_CAME, tile), have[FAR, tile], WIDE, outward)

    def near_out(tile):
        fly((NEAR_CAME, tile), have[NEAR, tile], WIDE, outward)

    def across(tile):
        far = add(have.pop((FAR, tile)), have.pop((FAR_CAME, tile)))
        fly((ACROSS, tile), far, WIDE, middle)

    def activate(tile):
        terms = [have.pop((key, tile)) for key in (NEAR, NEAR_CAME, ACROSS)]
        act = activated_sum(*terms, own_bias, PAD if tile == tiles - 1 else 0)
        put((ACT, tile), act)
        fly((FAR_ACT, tile), act, WIDE, middle)
        fly((NEAR_ACT, tile), act, WIDE, inward)

    def far_in(tile):
        fly((FAR_ACT_END, tile), have[FAR_ACT, tile], WIDE, inward)

    def near_product(tile):
        terms = [have[ACT, tile], have[NEAR_ACT, tile]]
        put((NEAR_VALUE, tile), near_product_of(place_at, second_weights(), *terms))

    def second_product(group):
        tile = group[0]
        if line == 4 and tile == tiles - 1:
            far, end = have.pop((FAR_ACT, tile)), have.pop((FAR_ACT_END, tile))
            value = have.pop((NEAR_VALUE, tile))
            out = far_product_of(place_at, second_weights(), far, end, value)
            del have[ACT, tile], have[NEAR_ACT, tile]
        elif line == 4:
            names = (ACT, NEAR_ACT, FAR_ACT, FAR_ACT_END)
            terms = [have.pop((name, tile)) for name in names]
            out = second_product_of(place_at, second_weights(), *terms)
        else:
            units = jnp.concatenate(have.pop((ACTS, tile)), axis=0)
            second = jnp.concatenate([second_columns(s) for s in starts], axis=1)
            value = jnp.dot(second, units, preferred_element_type=F32).astype(BF16)
            cut = value.shape[1] // 2
            out = value[:, :cut], value[:, cut:]
        put((VALUE, group), out[0])
        fly((PART, group), out[1], NARROW, 1)

    def halve(bit):
        def step(tile):
            if bit == 1:
                came = have.pop((CAME, ALL, tile))
                total = have.pop((OWN, tile)).astype(F32) + came.astype(F32)
            else:
                total = have.pop((SUM, tile)).astype(F32) + have.pop((PART, tile)).astype(F32)
            total = total.astype(BF16)
            cut = total.shape[0] // 2
            put((SUM, tile), total[:cut])
            put((PART, tile), swap(total[cut:], WIDE, 1 << bit))

        return step

    def double(bit):
        def step(tile):
            if bit == wide_bits - 1:
                total = have.pop((SUM, tile)).astype(F32) + have.pop((PART, tile)).astype(F32)
                act = jax.nn.gelu(total + own_bias, approximate=False).astype(BF16)
                put((ACTS, tile), [act])
            acts = have[ACTS, tile]
            put((ACTS, tile), acts + [swap(act, WIDE, 1 << bit) for act in acts])

        return step

    def narrow_step(group, bit):
        value, send = cut_sum(have[VALUE, group], have[PART, group])
        put((VALUE, group), value)
        fly((PART, group), send, NARROW, 1 << bit)

    def trade(group):
        done = finish(have[VALUE, group], have[PART, group], out_bias[1], 1)
        fly((TRADED, group), done, WIDE, 1)

    def keep(group):
        put((KEPT, group), finish(have.pop((VALUE, group)), have.pop((PART, group)), out_bias[0], 0))

    def steps_of(group):
        pairs = {}
        for tile in group:
            for step, some in moves[tile]:
                pairs[step] = sorted(set(pairs.get(step, []) + some))
        return dict(sorted(pairs.items()))

    def halo(group):
        whole = jnp.concatenate([have.pop((KEPT, group)), have.pop((TRADED, group))], axis=1)
        for step, pairs in steps_of(group).items():
            if step:
                fly((MOVED, step, group), whole, NARROW, pairs)
            else:
                put((MOVED, step, group), whole)

    def place(group):
        keys = [(MOVED, step, group) for step in steps_of(group)]
        moved = jnp.concatenate([have.pop(key) for key in keys], axis=1)
        more = jnp.dot(moved, have.pop((HITS, group)), preferred_element_type=F32)
        put((PLACED,), have[PLACED,] + more.astype(BF16))

    def late_second():
        fly((SECOND, 1), second_weight[early:], WIDE, 1)

    def order_first():
        if line == 4:
            put((FIRST,), turn(have[FIRST,], place_at[:1]))
        else:
            cut = [lax.dynamic_slice_in_dim(have[FIRST,], s, block, 1) for s in starts]
            put((FIRST,), jnp.concatenate(cut, axis=1).T)

    def spot_of(step, tile, half):
        whose = narrow_at - step
        at = (jnp.clip(whose, 0, narrow - 1) * tiles + tile) * TILE_ROWS + half * HALF
        spot = lax.dynamic_slice_in_dim(have[POS,], at, HALF, 0) - first_row
        return jnp.where((whose >= 0) & (whose < narrow), spot, -1)

    def clear_marked():
        marked = jnp.zeros((prompt_rows,), bool)
        for group in groups:
            steps = sorted({step for tile in group for step, _ in moves[tile]})
            spots = [
                spot_of(step, tile, half)
                for step in steps
                for half in (side_at, 1 - side_at)
                for tile in group
            ]
            found = jnp.concatenate(spots)[:, None] == grid
            marked |= jnp.any(found, axis=0)
            put((HITS, group), found.astype(BF16))
        put((PLACED,), jnp.where(marked[None, :], jnp.zeros((), BF16), have[PLACED,]))

    put((FIRST,), flat)
    put((PLACED,), text_embeds)
    put((POS,), vis_pos)
    fly((SECOND, 0), second_early, WIDE, 1)

    events = []

    def at(time, needs, step, *args):
        events.append((time, len(events), needs, step, args))

    parts = [FAR, NEAR] if line == 4 else [ALL]
    nothing = lambda: None
    at(19, [], norm_step, THEIRS, 0)
    at(20, [], gather_step, THEIRS, 0, HIGH)
    at(20.1, [], gather_step, THEIRS, 0, OWN)
    at(21, [], norm_step, MINE, 0)
    at(22, [], order_first)
    at(30, of(THEIRS, 0, HIGH), gather_step, THEIRS, 0, REST)
    at(31, [], gather_step, MINE, 0, HIGH)
    at(31.1, [], norm_step, BOTH, 1)
    at(31.2, [], gather_step, BOTH, 1, HIGH)
    needs = of(THEIRS, 0, OWN) + of(THEIRS, 0, REST) + [(SECOND, 0)]
    at(34, needs, send_theirs, 0, parts[0])
    at(34.1, [], fly_theirs, 0, parts[0])
    at(42, of(MINE, 0, HIGH), gather_step, MINE, 0, OWN)
    at(42.1, [], gather_step, MINE, 0, REST)
    if line == 4:
        at(42.2, [], send_theirs, 0, NEAR)
        at(42.3, [], fly_theirs, 0, NEAR)
    at(45, of(MINE, 0, OWN) + of(MINE, 0, REST), keep_mine, 0)
    for tile in range(2, tiles):
        at(45.1 + 0.1 * tile, [], norm_step, BOTH, tile)
    tick = 19.5
    for tile in range(1, tiles):
        arrived = 65 + tick * (tile - 1) + 0.4
        if tile == 1:
            at(arrived, [], gather_step, BOTH, 1, OWN)
        at(arrived, of(BOTH, tile, HIGH), gather_step, BOTH, tile, REST)
        if tile + 1 < tiles:
            at(arrived + 0.1, [], gather_step, BOTH, tile + 1, HIGH)
            at(arrived + 0.2, [], gather_step, BOTH, tile + 1, OWN)
        needs = of(BOTH, tile, OWN) + of(BOTH, tile, REST)
        at(68 if tile == 1 else 65 + tick * tile - 0.1, needs, nothing)
        at(68.1 if tile == 1 else 65 + tick * (2 * tile - 2) + 1, [], send_and_keep, tile)
    last = 65 + tick * (2 * tiles - 1)
    at(65 + tick + 2, [], clear_marked)
    at(last + 0.2, [], late_second)
    for tile in range(tiles):
        if line == 4:
            a = 65 + tick * (2 * tile + 1)
            b = a + tick
            if tile == 0:
                at(a - tick, [(CAME, FAR, 0)], far_ready, 0)
                at(a - tick, [], far_out, 0)
            at(a, [(CAME, NEAR, tile)], near_ready, tile)
            at(a + 0.1, [(FAR_CAME, tile)], near_out, tile)
            at(a + 0.1, [], across, tile)
            if tile + 1 < tiles:
                at(b, [(CAME, FAR, tile + 1)], far_ready, tile + 1)
            at(b + 0.1, [(NEAR_CAME, tile)], far_out, tile + 1)
            at(b + 0.2, [(ACROSS, tile)], activate, tile)
            at(b + tick + 0.3, [(FAR_ACT, tile), (NEAR_ACT, tile)], far_in, tile)
            at(b + 2 * tick + 0.3, [(FAR_ACT_END, tile)], nothing)
        else:
            base = 74 + 37 * tile
            for i, bit in enumerate(range(1, wide_bits)):
                needs = [(PART, tile)] if i else [(CAME, ALL, tile)]
                at(base + 8 * i, needs, halve(bit), tile)
            for i, bit in enumerate(reversed(range(1, wide_bits))):
                needs = [] if i else [(PART, tile)]
                at(base + 35 + 8 * i, needs, double(bit), tile)
    done = last + 3 * tick + 0.4
    at(done - 2 * tick + 4, [(SECOND, 1)], join_second)
    if line == 4:
        at(done - 12, [], near_product, tiles - 1)
    for i, group in enumerate(groups):
        if line == 4 and tiles == 4:
            times = (
                (-34, -19, -6, 5, 13),
                (-33, -18.9, 3, 12.5, 21),
                (-18.8, 1, 12, 20.5, 28),
                (0, 4, 20, 27, 31),
            )[i]
        else:
            times = (10 * i, 10 * i + 1, 10 * i + 5, 10 * i + 6, 10 * i + 7)
        times = [done + time for time in times]
        at(times[0], [], second_product, group)
        for bit in range(1, narrow_bits):
            at(times[1] + 0.1 * bit, [(PART, group)], narrow_step, group, bit)
        at(times[2], [(PART, group)], trade, group)
        at(times[2] + 0.1, [], keep, group)
        at(times[3], [(TRADED, group)], halo, group)
        flown = [(MOVED, step, group) for step in steps_of(group) if step]
        at(times[4], flown, place, group)
    for _, _, needs, step, args in sorted(events, key=lambda e: e[:2]):
        sync(needs)
        step(*args)
    return have[PLACED,]


def solution(mesh):
    in_specs = (
        P(WIDE, NARROW),
        P(None, WIDE),
        P(None, WIDE),
        P(None, WIDE, NARROW),
        P(NARROW),
        P(WIDE, NARROW),
        P(WIDE),
        P(WIDE, NARROW),
        P(),
    )
    out_specs = P(WIDE, NARROW)
    return jax.shard_map(shards, mesh=mesh, in_specs=in_specs, out_specs=out_specs, check_vma=False)
```

```python
import functools

import jax
import jax.numpy as jnp
from jax import lax
from jax.experimental import pallas as pl
from jax.experimental.pallas import tpu as pltpu
from jax.sharding import PartitionSpec as P

D = 3200
TILE_SIDE = 32
TILE_ROWS = 256
HALF = 128
COLS = 512
PAD = 16
STEP = 256
F32 = jnp.float32
BF16 = jnp.bfloat16
WIDE, NARROW = "wide", "narrow"
(
    SENT,
    HIGH,
    OWN,
    THEIRS,
    MINE,
    BOTH,
    ALL,
    FIRST,
    NEAR,
    CAME,
    FAR,
    SECOND,
    FAR_CAME,
    NEAR_CAME,
    ACROSS,
    ACT,
    FAR_ACT,
    NEAR_ACT,
    FAR_ACT_END,
    NEAR_VALUE,
    ACTS,
    VALUE,
    PART,
    SUM,
    TRADED,
    KEPT,
    MOVED,
    PLACED,
    REST,
    HITS,
    POS,
) = range(31)


def bit_reversed(bits):
    return [sum(((p >> b) & 1) << (bits - 1 - b) for b in range(bits)) for p in range(1 << bits)]


def swap(value, axis, mask):
    count = lax.axis_size(axis)
    return lax.ppermute(value, axis, [(i, i ^ mask) for i in range(count)])


def merge_kernel(patch_ref, order_ref, *refs):
    merged_refs, stats_ref = refs[:-1], refs[-1]
    mixed = jnp.dot(patch_ref[...], order_ref[...], preferred_element_type=F32)
    total = jnp.zeros((1, HALF), F32)
    squares = jnp.zeros((1, HALF), F32)
    for slot in range(4):
        part = mixed[:, slot * HALF : (slot + 1) * HALF]
        total += jnp.sum(part, axis=0, keepdims=True)
        squares += jnp.sum(part * part, axis=0, keepdims=True)
    stats_ref[0:1, :] = total
    stats_ref[1:2, :] = squares
    for tile, merged_ref in enumerate(merged_refs):

        @pl.when(pl.program_id(0) // 2 == tile)
        def _():
            for slot in range(4):
                merged_ref[0, slot] = mixed[:, slot * HALF : (slot + 1) * HALF].astype(BF16)


def merge(patches):
    columns, width = patches.shape
    steps = width // COLS
    side = TILE_SIDE // 2
    source = lax.broadcasted_iota(jnp.int32, (COLS, COLS), 0)
    target = lax.broadcasted_iota(jnp.int32, (COLS, COLS), 1)
    slot = target // HALF
    row = target % HALF
    wanted = (
        (row // side) * (4 * side) + (slot // 2) * (2 * side) + (row % side) * 2 + slot % 2
    )
    order = (source == wanted).astype(BF16)

    def tile_spec(tile):
        return pl.BlockSpec(
            (1, 4, columns, HALF), lambda i: (jnp.clip(i - 2 * tile, 0, 1), 0, 0, 0)
        )

    tiles = steps // 2
    out = pl.pallas_call(
        merge_kernel,
        grid=(steps,),
        in_specs=[
            pl.BlockSpec((columns, COLS), lambda i: (0, i)),
            pl.BlockSpec((COLS, COLS), lambda i: (0, 0)),
        ],
        out_specs=[tile_spec(tile) for tile in range(tiles)]
        + [pl.BlockSpec((2, HALF), lambda i: (0, i))],
        out_shape=[jax.ShapeDtypeStruct((2, 4, columns, HALF), BF16)] * tiles
        + [jax.ShapeDtypeStruct((2, steps * HALF), F32)],
        compiler_params=pltpu.CompilerParams(vmem_limit_bytes=24 * 1024 * 1024),
    )(patches, order)
    return out[:-1], out[-1]


def call(kernel, grid, in_specs, out_specs, out_shape, scratch_shapes=(), scalars=0, flops=1):
    return pl.pallas_call(
        kernel,
        grid_spec=pltpu.PrefetchScalarGridSpec(
            num_scalar_prefetch=scalars,
            grid=grid,
            in_specs=in_specs,
            out_specs=out_specs,
            scratch_shapes=scratch_shapes,
        ),
        out_shape=out_shape,
        cost_estimate=pl.CostEstimate(flops=flops, bytes_accessed=1, transcendentals=0),
        compiler_params=pltpu.CompilerParams(vmem_limit_bytes=24 * 1024 * 1024),
    )


def like(rows, width):
    return jax.ShapeDtypeStruct((rows, width), BF16)


def norm_kernel(half_ref, merged_ref, mean_ref, scale_ref, gain_ref, shift_ref, out_ref):
    for slot in range(4):
        values = merged_ref[0, slot].astype(F32)
        gain, shift = gain_ref[:, slot : slot + 1], shift_ref[:, slot : slot + 1]
        result = (values - mean_ref[...]) * scale_ref[...] * gain + shift
        out_ref[slot] = result.astype(BF16)


def norm(merged, mean, scale, gain, shift, tile, halves):
    columns = merged.shape[2]
    out = call(
        norm_kernel,
        (len(halves),),
        [
            pl.BlockSpec((1, 4, columns, HALF), lambda i, h: (h[i], 0, 0, 0)),
            pl.BlockSpec((1, HALF), lambda i, h: (0, h[i] + 2 * tile)),
            pl.BlockSpec((1, HALF), lambda i, h: (0, h[i] + 2 * tile)),
            pl.BlockSpec((columns, 4), lambda i, h: (0, 0)),
            pl.BlockSpec((columns, 4), lambda i, h: (0, 0)),
        ],
        pl.BlockSpec((4, columns, HALF), lambda i, h: (0, 0, i)),
        jax.ShapeDtypeStruct((4, columns, len(halves) * HALF), BF16),
        scalars=1,
    )(jnp.stack(halves).astype(jnp.int32), merged, mean, scale, gain, shift)
    return [out.reshape(-1, len(halves) * HALF)]


def turn_kernel(first_ref, flat_ref, out_ref):
    out_ref[...] = flat_ref[...].T


def turn(flat, near):
    depth, hidden = flat.shape
    step = 256
    half = hidden // 2 // step
    return call(
        turn_kernel,
        (2 * half,),
        [pl.BlockSpec((depth, step), lambda i, n: (0, (i // half + n[0]) % 2 * half + i % half))],
        pl.BlockSpec((step, depth), lambda i, n: (i, 0)),
        like(hidden, depth),
        scalars=1,
    )(near, flat)


def whole(kernel, out_shape, scratch_shapes=(), scalars=0, count=0):
    specs = [pl.BlockSpec(memory_space=pltpu.SMEM)] * scalars
    specs += [pl.BlockSpec(memory_space=pltpu.VMEM)] * count
    return pl.pallas_call(
        kernel,
        in_specs=specs,
        out_specs=[pl.BlockSpec(memory_space=pltpu.VMEM)] * len(out_shape),
        out_shape=out_shape,
        scratch_shapes=scratch_shapes,
        cost_estimate=pl.CostEstimate(flops=1, bytes_accessed=1, transcendentals=0),
        compiler_params=pltpu.CompilerParams(vmem_limit_bytes=24 * 1024 * 1024),
    )


def product_kernel(half, start, weight_ref, *refs):
    tile_refs, out_ref, rows_ref = refs[:-2], refs[-2], refs[-1]
    for i, tile_ref in enumerate(tile_refs):
        columns = slice(half * HALF, (half + 1) * HALF)
        rows_ref[:, i * HALF : (i + 1) * HALF] = tile_ref[:, columns]
    rows = out_ref.shape[0]
    step = STEP if rows % STEP == 0 else rows
    for row in range(0, rows, step):
        weight = weight_ref[start + row : start + row + step, :]
        out = jnp.dot(weight, rows_ref[...], preferred_element_type=F32)
        out_ref[row : row + step, :] = out.astype(BF16)


def product(weight, tiles, half, start, rows):
    width = len(tiles) * HALF
    return whole(
        functools.partial(product_kernel, half, start),
        [like(rows, width)],
        [pltpu.VMEM((weight.shape[1], width), BF16)],
        count=1 + len(tiles),
    )(weight, *[tile[0] for tile in tiles])[0]


def products_kernel(weight_ref, *refs):
    tile_refs, (near_ref, far_ref, own_ref, rows_ref) = refs[:-4], refs[-4:]
    width = len(tile_refs) * HALF
    for i, tile_ref in enumerate(tile_refs):
        place = slice(i * HALF, (i + 1) * HALF)
        rows_ref[:, place] = tile_ref[:, :HALF]
        rows_ref[:, slice(width + i * HALF, width + (i + 1) * HALF)] = tile_ref[:, HALF:]
    half = near_ref.shape[0]
    step = STEP
    for row in range(0, 2 * half, step):
        some = slice(row, row + step)
        out = jnp.dot(weight_ref[some, :], rows_ref[...], preferred_element_type=F32).astype(BF16)
        own_ref[some, :] = out[:, width:]
        if row < half:
            near_ref[some, :] = out[:, :width]
        else:
            far_ref[row - half : row - half + step, :] = out[:, :width]


def products(weight, tiles):
    rows, depth = weight.shape
    width = len(tiles) * HALF
    return whole(
        products_kernel,
        [like(rows // 2, width), like(rows // 2, width), like(rows, width)],
        [pltpu.VMEM((depth, 2 * width), BF16)],
        count=1 + len(tiles),
    )(weight, *[tile[0] for tile in tiles])


def add_kernel(start, one_ref, other_ref, out_ref):
    rows = out_ref.shape[0]
    one = one_ref[start : start + rows, :].astype(F32)
    out_ref[...] = (one + other_ref[...].astype(F32)).astype(BF16)


def add(one, other, start=0):
    kernel = functools.partial(add_kernel, start)
    return whole(kernel, [like(*other.shape)], count=2)(one, other)[0]


def activate_kernel(one_ref, two_ref, three_ref, bias_ref, out_ref):
    rows = one_ref.shape[0]
    step = rows // 4
    for i in range(4):
        some = slice(i * step, (i + 1) * step)
        total = one_ref[some, :].astype(F32) + two_ref[some, :].astype(F32)
        total = total + three_ref[some, :].astype(F32) + bias_ref[some, :]
        out_ref[some, :] = (0.5 * total * (1.0 + lax.erf(total * 0.5**0.5))).astype(BF16)
    if out_ref.shape[0] > rows:
        out_ref[rows:, :] = jnp.zeros((out_ref.shape[0] - rows, out_ref.shape[1]), BF16)


def activated_sum(one, two, three, bias, pad):
    rows, width = one.shape
    return whole(activate_kernel, [like(rows + pad, width)], count=4)(one, two, three, bias)[0]


def second_kernel(place_ref, own_weight_ref, other_weight_ref, own_ref, near_ref, far_ref, end_ref, keep_ref, send_ref, units_ref):
    half = own_weight_ref.shape[1] // 2
    rows = own_weight_ref.shape[0]
    near_at = place_ref[0] * half

    @pl.when(place_ref[1] == 1)
    def _():
        units_ref[pl.ds(near_at, half), :] = own_ref[:half, :]
        units_ref[pl.ds(half - near_at, half), :] = far_ref[:half, :]

    @pl.when(place_ref[1] == 0)
    def _():
        units_ref[pl.ds(near_at, half), :] = near_ref[:half, :]
        units_ref[pl.ds(half - near_at, half), :] = end_ref[:half, :]

    cut = keep_ref.shape[1]
    for i, ref in enumerate((own_weight_ref, other_weight_ref)):
        for row in range(0, rows, STEP):
            out = jnp.dot(ref[row : row + STEP, :], units_ref[...], preferred_element_type=F32)
            some = slice(i * rows + row, i * rows + row + STEP)
            keep_ref[some, :] = out[:, :cut].astype(BF16)
            send_ref[some, :] = out[:, cut:].astype(BF16)


def second_product_of(place, weights, own, near, far, end):
    rows, depth = weights[0].shape
    width = own.shape[1]
    return whole(
        second_kernel,
        [like(2 * rows, width // 2)] * 2,
        [pltpu.VMEM((depth, width), BF16)],
        scalars=1,
        count=6,
    )(place, *weights, own, near, far, end)


def near_kernel(place_ref, own_weight_ref, other_weight_ref, own_ref, near_ref, value_ref, units_ref):
    half = units_ref.shape[0]
    rows = own_weight_ref.shape[0]

    @pl.when(place_ref[1] == 1)
    def _():
        units_ref[...] = own_ref[:half, :]

    @pl.when(place_ref[1] == 0)
    def _():
        units_ref[...] = near_ref[:half, :]

    columns = pl.ds(pl.multiple_of(place_ref[0] * half, HALF), half)
    for i, ref in enumerate((own_weight_ref, other_weight_ref)):
        for row in range(0, rows, STEP):
            weight = ref[row : row + STEP, columns]
            out = jnp.dot(weight, units_ref[...], preferred_element_type=F32)
            value_ref[i * rows + row : i * rows + row + STEP, :] = out


def near_product_of(place, weights, own, near):
    rows, depth = weights[0].shape
    width = near.shape[1]
    return whole(
        near_kernel,
        [jax.ShapeDtypeStruct((2 * rows, width), F32)],
        [pltpu.VMEM((depth // 2, width), BF16)],
        scalars=1,
        count=4,
    )(place, *weights, own, near)[0]


def far_kernel(place_ref, own_weight_ref, other_weight_ref, far_ref, end_ref, value_ref, keep_ref, send_ref, units_ref):
    half = units_ref.shape[0]
    rows = own_weight_ref.shape[0]

    @pl.when(place_ref[1] == 1)
    def _():
        units_ref[...] = far_ref[:half, :]

    @pl.when(place_ref[1] == 0)
    def _():
        units_ref[...] = end_ref[:half, :]

    cut = keep_ref.shape[1]
    columns = pl.ds(pl.multiple_of(half - place_ref[0] * half, HALF), half)
    for i, ref in enumerate((own_weight_ref, other_weight_ref)):
        for row in range(0, rows, STEP):
            some = slice(i * rows + row, i * rows + row + STEP)
            weight = ref[row : row + STEP, columns]
            out = jnp.dot(weight, units_ref[...], preferred_element_type=F32) + value_ref[some, :]
            keep_ref[some, :] = out[:, :cut].astype(BF16)
            send_ref[some, :] = out[:, cut:].astype(BF16)


def far_product_of(place, weights, far, end, value):
    rows, depth = weights[0].shape
    width = far.shape[1]
    return whole(
        far_kernel,
        [like(2 * rows, width // 2)] * 2,
        [pltpu.VMEM((depth // 2, width), BF16)],
        scalars=1,
        count=5,
    )(place, *weights, far, end, value)


def cut_kernel(one_ref, other_ref, keep_ref, send_ref):
    total = (one_ref[...].astype(F32) + other_ref[...].astype(F32)).astype(BF16)
    cut = keep_ref.shape[1]
    keep_ref[...] = total[:, :cut]
    send_ref[...] = total[:, cut:]


def cut_sum(one, other):
    rows, width = one.shape
    return whole(cut_kernel, [like(rows, width // 2)] * 2, count=2)(one, other)


def finish_kernel(start, one_ref, two_ref, bias_ref, out_ref):
    some = slice(start, start + out_ref.shape[0])
    total = one_ref[some, :].astype(F32) + two_ref[some, :].astype(F32)
    out_ref[...] = (total + bias_ref[...]).astype(BF16)


def finish(one, two, bias, half):
    rows = bias.shape[0]
    kernel = functools.partial(finish_kernel, half * rows)
    return whole(kernel, [like(rows, one.shape[1])], count=3)(one, two, bias)[0]


def shards(
    patches,
    ln_gain,
    ln_bias,
    first_weight,
    first_bias,
    second_weight,
    second_bias,
    text_embeds,
    vis_pos,
):
    wide = lax.axis_size(WIDE)
    narrow = lax.axis_size(NARROW)
    wide_bits = wide.bit_length() - 1
    narrow_bits = narrow.bit_length() - 1
    line = wide // 2
    wide_at = lax.axis_index(WIDE)
    narrow_at = lax.axis_index(NARROW)
    side_at = wide_at % 2
    line_at = wide_at // 2
    columns = patches.shape[0]
    hidden = first_weight.shape[2]
    features = second_weight.shape[0]
    tiles = patches.shape[1] // (4 * TILE_ROWS)
    prompt_rows = text_embeds.shape[1]
    depth = 4 * columns
    block = hidden // line

    merged, stats = merge(patches)
    other_bias = swap(second_bias, WIDE, 1)
    stats = stats + swap(stats, WIDE, 1)
    early = features // 2 // 16 * 16
    gain = ln_gain.astype(F32).T
    shift = ln_bias.astype(F32).T
    second_early = second_weight[:early]
    stats, second_early, other_bias, gain, shift = lax.optimization_barrier(
        (stats, second_early, other_bias, gain, shift)
    )
    for bit in range(1, wide_bits):
        stats = stats + swap(stats, WIDE, 1 << bit)
    entries = 4.0 * D
    row_mean = stats[0] / entries
    row_var = stats[1] / entries - row_mean * row_mean
    inverse = lax.rsqrt(row_var + 1e-05)
    def normed(tile, halves):
        return norm(merged[tile], row_mean[None, :], inverse[None, :], gain, shift, tile, halves)

    if line == 4:
        starts = [(line_at // 2 ^ i) * (hidden // 2) for i in range(2)]
    else:
        starts = [(line_at ^ i) * (hidden // line) for i in bit_reversed(wide_bits - 1)]
    block = hidden // len(starts)
    flat = first_weight.reshape(depth, hidden)
    own_bias = lax.dynamic_slice_in_dim(first_bias, starts[0], block, 0).astype(F32)[:, None]
    out_bias = [bias.astype(F32)[:, None] for bias in (second_bias, other_bias)]

    text_rows = narrow * prompt_rows - vis_pos.shape[0]
    first_row = narrow_at * prompt_rows
    grid = jnp.arange(prompt_rows, dtype=jnp.int32)[None, :]
    moves = {tile: [] for tile in range(tiles)}
    for tile in range(tiles):
        for step in range(1 - narrow, narrow):
            pairs = []
            for source in range(narrow):
                target = source + step
                low = (source * tiles + tile) * TILE_ROWS
                if (
                    0 <= target < narrow
                    and low < (target + 1) * prompt_rows
                    and low + text_rows + TILE_ROWS > target * prompt_rows
                ):
                    pairs.append((source, target))
            if pairs:
                moves[tile].append((step, pairs))
    groups = [(t,) for t in range(tiles)]

    tile_order = bit_reversed(narrow_bits)
    outward = [(x, 2 + x) for x in (0, 1)] + [(6 + x, 4 + x) for x in (0, 1)]
    inward = [(b, a) for a, b in outward]
    middle = [(2 + x, 4 + x) for x in (0, 1)] + [(4 + x, 2 + x) for x in (0, 1)]
    is_middle = (line_at == 1) | (line_at == 2)
    place_at = jnp.stack([line_at // 2 % 2, is_middle.astype(jnp.int32)]).astype(jnp.int32)
    have, joined = {}, set()

    def put(key, value, flying=False):
        have[key] = value
        joined.discard(key)
        if not flying:
            joined.add(key)

    def fly(key, value, axis, pairs):
        if isinstance(pairs, int):
            pairs = [(i, i ^ pairs) for i in range(lax.axis_size(axis))]
        put(key, lax.ppermute(value, axis, pairs), True)
        put((SENT, key), value)

    def sync(needs):
        joined.update(needs)
        keys = [k for k in have if k in joined]
        have.update(zip(keys, lax.optimization_barrier([have[k] for k in keys])))
        for key in keys:
            if key[0] == SENT:
                del have[key]

    def hops(key, tile, stage):
        if stage == HIGH:
            return [(key, 0, narrow // 2, tile)]
        base = 0 if stage == OWN else narrow // 2
        found, result = [base], []
        for bit in reversed(range(narrow_bits - 1)):
            result += [(key, d, d + (1 << bit), tile) for d in found]
            found += [d + (1 << bit) for d in found]
        return result

    row_parts = 1

    def of(key, tile, stage):
        return [
            (key, to, tile, part)
            for key, _, to, tile in hops(key, tile, stage)
            for part in range(row_parts)
        ]

    def norm_step(key, tile):
        theirs, mine = 1 - side_at, side_at
        halves = {THEIRS: [theirs], MINE: [mine], BOTH: [theirs, mine]}[key]
        for part, value in enumerate(normed(tile, halves)):
            put((key, 0, tile, part), value)

    def gather_step(key, tile, stage):
        for key, origin, to, tile in hops(key, tile, stage):
            for part in range(row_parts):
                fly((key, to, tile, part), have[key, origin, tile, part], NARROW, origin ^ to)

    def pieces_of(key, tile):
        return [[have[key, d, tile, part] for part in range(row_parts)] for d in tile_order]

    def drop(tile):
        for key in [key for key in have if len(key) == 4 and key[2] == tile]:
            del have[key]

    def send_theirs(tile, part):
        key = BOTH if tile else THEIRS
        pieces = pieces_of(key, tile)
        if part == ALL:
            sent = product(have[FIRST,], pieces, 0, 0, hidden)
        else:
            sent = product(have[FIRST,], pieces, 0, 0 if part == NEAR else block, block)
        put((THEIRS, part, tile), sent)

    def fly_theirs(tile, part):
        if tile < tiles:
            fly((CAME, part, tile), have.pop((THEIRS, part, tile)), WIDE, 1)

    def send_and_keep(tile):
        if line == 4:
            near, far, own = products(have[FIRST,], pieces_of(BOTH, tile))
            put((THEIRS, NEAR, tile), near)
            put((THEIRS, FAR, tile), far)
            put((OWN, tile), own)
            drop(tile)
        else:
            send_theirs(tile, ALL)
            fly_theirs(tile, ALL)
            keep_mine(tile)

    def keep_mine(tile):
        key = BOTH if tile else MINE
        own = product(have[FIRST,], pieces_of(key, tile), 1 if tile else 0, 0, hidden)
        put((OWN, tile), own)
        drop(tile)

    def second_weights():
        return [second_weight, have[SECOND,]]

    def second_columns(at):
        parts = [lax.dynamic_slice_in_dim(part, at, block, 1) for part in second_weights()]
        return jnp.concatenate(parts, axis=0)

    def join_second():
        parts = [have.pop((SECOND, 0)), have.pop((SECOND, 1))]
        put((SECOND,), jnp.concatenate(parts, axis=0))

    def far_ready(tile):
        if tile:
            fly_theirs(tile, NEAR)
        put((FAR, tile), add(have[OWN, tile], have.pop((CAME, FAR, tile)), block))

    def near_ready(tile):
        fly_theirs(tile + 1, FAR)
        put((NEAR, tile), add(have.pop((OWN, tile)), have.pop((CAME, NEAR, tile))))

    def far_out(tile):
        if tile < tiles:
            fly((FAR_CAME, tile), have[FAR, tile], WIDE, outward)

    def near_out(tile):
        fly((NEAR_CAME, tile), have[NEAR, tile], WIDE, outward)

    def across(tile):
        far = add(have.pop((FAR, tile)), have.pop((FAR_CAME, tile)))
        fly((ACROSS, tile), far, WIDE, middle)

    def activate(tile):
        terms = [have.pop((key, tile)) for key in (NEAR, NEAR_CAME, ACROSS)]
        act = activated_sum(*terms, own_bias, PAD if tile == tiles - 1 else 0)
        put((ACT, tile), act)
        fly((FAR_ACT, tile), act, WIDE, middle)
        fly((NEAR_ACT, tile), act, WIDE, inward)

    def far_in(tile):
        fly((FAR_ACT_END, tile), have[FAR_ACT, tile], WIDE, inward)

    def near_product(tile):
        terms = [have[ACT, tile], have[NEAR_ACT, tile]]
        put((NEAR_VALUE, tile), near_product_of(place_at, second_weights(), *terms))

    def second_product(group):
        tile = group[0]
        if line == 4 and tile == tiles - 1:
            far, end = have.pop((FAR_ACT, tile)), have.pop((FAR_ACT_END, tile))
            value = have.pop((NEAR_VALUE, tile))
            out = far_product_of(place_at, second_weights(), far, end, value)
            del have[ACT, tile], have[NEAR_ACT, tile]
        elif line == 4:
            names = (ACT, NEAR_ACT, FAR_ACT, FAR_ACT_END)
            terms = [have.pop((name, tile)) for name in names]
            out = second_product_of(place_at, second_weights(), *terms)
        else:
            units = jnp.concatenate(have.pop((ACTS, tile)), axis=0)
            second = jnp.concatenate([second_columns(s) for s in starts], axis=1)
            value = jnp.dot(second, units, preferred_element_type=F32).astype(BF16)
            cut = value.shape[1] // 2
            out = value[:, :cut], value[:, cut:]
        put((VALUE, group), out[0])
        fly((PART, group), out[1], NARROW, 1)

    def halve(bit):
        def step(tile):
            if bit == 1:
                came = have.pop((CAME, ALL, tile))
                total = have.pop((OWN, tile)).astype(F32) + came.astype(F32)
            else:
                total = have.pop((SUM, tile)).astype(F32) + have.pop((PART, tile)).astype(F32)
            total = total.astype(BF16)
            cut = total.shape[0] // 2
            put((SUM, tile), total[:cut])
            put((PART, tile), swap(total[cut:], WIDE, 1 << bit))

        return step

    def double(bit):
        def step(tile):
            if bit == wide_bits - 1:
                total = have.pop((SUM, tile)).astype(F32) + have.pop((PART, tile)).astype(F32)
                act = jax.nn.gelu(total + own_bias, approximate=False).astype(BF16)
                put((ACTS, tile), [act])
            acts = have[ACTS, tile]
            put((ACTS, tile), acts + [swap(act, WIDE, 1 << bit) for act in acts])

        return step

    def narrow_step(group, bit):
        value, send = cut_sum(have[VALUE, group], have[PART, group])
        put((VALUE, group), value)
        fly((PART, group), send, NARROW, 1 << bit)

    def trade(group):
        done = finish(have[VALUE, group], have[PART, group], out_bias[1], 1)
        fly((TRADED, group), done, WIDE, 1)

    def keep(group):
        put((KEPT, group), finish(have.pop((VALUE, group)), have.pop((PART, group)), out_bias[0], 0))

    def steps_of(group):
        pairs = {}
        for tile in group:
            for step, some in moves[tile]:
                pairs[step] = sorted(set(pairs.get(step, []) + some))
        return dict(sorted(pairs.items()))

    def halo(group):
        whole = jnp.concatenate([have.pop((KEPT, group)), have.pop((TRADED, group))], axis=1)
        for step, pairs in steps_of(group).items():
            if step:
                fly((MOVED, step, group), whole, NARROW, pairs)
            else:
                put((MOVED, step, group), whole)

    def place(group):
        keys = [(MOVED, step, group) for step in steps_of(group)]
        moved = jnp.concatenate([have.pop(key) for key in keys], axis=1)
        more = jnp.dot(moved, have.pop((HITS, group)), preferred_element_type=F32)
        put((PLACED,), have[PLACED,] + more.astype(BF16))

    def late_second():
        fly((SECOND, 1), second_weight[early:], WIDE, 1)

    def order_first():
        if line == 4:
            put((FIRST,), turn(have[FIRST,], place_at[:1]))
        else:
            cut = [lax.dynamic_slice_in_dim(have[FIRST,], s, block, 1) for s in starts]
            put((FIRST,), jnp.concatenate(cut, axis=1).T)

    def spot_of(step, tile, half):
        whose = narrow_at - step
        at = (jnp.clip(whose, 0, narrow - 1) * tiles + tile) * TILE_ROWS + half * HALF
        spot = lax.dynamic_slice_in_dim(have[POS,], at, HALF, 0) - first_row
        return jnp.where((whose >= 0) & (whose < narrow), spot, -1)

    def clear_marked():
        marked = jnp.zeros((prompt_rows,), bool)
        for group in groups:
            steps = sorted({step for tile in group for step, _ in moves[tile]})
            spots = [
                spot_of(step, tile, half)
                for step in steps
                for half in (side_at, 1 - side_at)
                for tile in group
            ]
            found = jnp.concatenate(spots)[:, None] == grid
            marked |= jnp.any(found, axis=0)
            put((HITS, group), found.astype(BF16))
        put((PLACED,), jnp.where(marked[None, :], jnp.zeros((), BF16), have[PLACED,]))

    put((FIRST,), flat)
    put((PLACED,), text_embeds)
    put((POS,), vis_pos)
    fly((SECOND, 0), second_early, WIDE, 1)

    events = []

    def at(time, needs, step, *args):
        events.append((time, len(events), needs, step, args))

    parts = [FAR, NEAR] if line == 4 else [ALL]
    nothing = lambda: None
    at(19, [], norm_step, THEIRS, 0)
    at(20, [], gather_step, THEIRS, 0, HIGH)
    at(20.1, [], gather_step, THEIRS, 0, OWN)
    at(21, [], norm_step, MINE, 0)
    at(22, [], order_first)
    at(30, of(THEIRS, 0, HIGH), gather_step, THEIRS, 0, REST)
    at(31, [], gather_step, MINE, 0, HIGH)
    at(31.1, [], norm_step, BOTH, 1)
    at(31.2, [], gather_step, BOTH, 1, HIGH)
    needs = of(THEIRS, 0, OWN) + of(THEIRS, 0, REST) + [(SECOND, 0)]
    at(34, needs, send_theirs, 0, parts[0])
    at(34.1, [], fly_theirs, 0, parts[0])
    at(42, of(MINE, 0, HIGH), gather_step, MINE, 0, OWN)
    at(42.1, [], gather_step, MINE, 0, REST)
    if line == 4:
        at(42.2, [], send_theirs, 0, NEAR)
        at(42.3, [], fly_theirs, 0, NEAR)
    at(45, of(MINE, 0, OWN) + of(MINE, 0, REST), keep_mine, 0)
    for tile in range(2, tiles):
        at(45.1 + 0.1 * tile, [], norm_step, BOTH, tile)
    tick = 19.5
    for tile in range(1, tiles):
        arrived = 65 + tick * (tile - 1) + 0.4
        if tile == 1:
            at(arrived, [], gather_step, BOTH, 1, OWN)
        at(arrived, of(BOTH, tile, HIGH), gather_step, BOTH, tile, REST)
        if tile + 1 < tiles:
            at(arrived + 0.1, [], gather_step, BOTH, tile + 1, HIGH)
            at(arrived + 0.2, [], gather_step, BOTH, tile + 1, OWN)
        needs = of(BOTH, tile, OWN) + of(BOTH, tile, REST)
        at(68 if tile == 1 else 65 + tick * tile - 0.1, needs, nothing)
        at(68.1 if tile == 1 else 65 + tick * (2 * tile - 2) + 1, [], send_and_keep, tile)
    last = 65 + tick * (2 * tiles - 1)
    at(65 + 3 * tick + 3, [], clear_marked)
    at(last + 0.2, [], late_second)
    for tile in range(tiles):
        if line == 4:
            a = 65 + tick * (2 * tile + 1)
            b = a + tick
            if tile == 0:
                at(a - tick, [(CAME, FAR, 0)], far_ready, 0)
                at(a - tick, [], far_out, 0)
            at(a, [(CAME, NEAR, tile)], near_ready, tile)
            at(a + 0.1, [(FAR_CAME, tile)], near_out, tile)
            at(a + 0.1, [], across, tile)
            if tile + 1 < tiles:
                at(b, [(CAME, FAR, tile + 1)], far_ready, tile + 1)
            at(b + 0.1, [(NEAR_CAME, tile)], far_out, tile + 1)
            at(b + 0.2, [(ACROSS, tile)], activate, tile)
            at(b + tick + 0.3, [(FAR_ACT, tile), (NEAR_ACT, tile)], far_in, tile)
            at(b + 2 * tick + 0.3, [(FAR_ACT_END, tile)], nothing)
        else:
            base = 74 + 37 * tile
            for i, bit in enumerate(range(1, wide_bits)):
                needs = [(PART, tile)] if i else [(CAME, ALL, tile)]
                at(base + 8 * i, needs, halve(bit), tile)
            for i, bit in enumerate(reversed(range(1, wide_bits))):
                needs = [] if i else [(PART, tile)]
                at(base + 35 + 8 * i, needs, double(bit), tile)
    done = last + 3 * tick + 0.4
    at(done - 2 * tick + 4, [(SECOND, 1)], join_second)
    if line == 4:
        at(done - 12, [], near_product, tiles - 1)
    for i, group in enumerate(groups):
        if line == 4 and tiles == 4:
            times = (
                (-34, -19, -6, 5, 13),
                (-33, -18.9, 3, 12.5, 21),
                (-18.8, 1, 12, 20.5, 28),
                (0, 4, 20, 27, 31),
            )[i]
        else:
            times = (10 * i, 10 * i + 1, 10 * i + 5, 10 * i + 6, 10 * i + 7)
        times = [done + time for time in times]
        at(times[0], [], second_product, group)
        for bit in range(1, narrow_bits):
            at(times[1] + 0.1 * bit, [(PART, group)], narrow_step, group, bit)
        at(times[2], [(PART, group)], trade, group)
        at(times[2] + 0.1, [], keep, group)
        at(times[3], [(TRADED, group)], halo, group)
        flown = [(MOVED, step, group) for step in steps_of(group) if step]
        at(times[4], flown, place, group)
    for _, _, needs, step, args in sorted(events, key=lambda e: e[:2]):
        sync(needs)
        step(*args)
    return have[PLACED,]


def solution(mesh):
    in_specs = (
        P(WIDE, NARROW),
        P(None, WIDE),
        P(None, WIDE),
        P(None, WIDE, NARROW),
        P(NARROW),
        P(WIDE, NARROW),
        P(WIDE),
        P(WIDE, NARROW),
        P(),
    )
    out_specs = P(WIDE, NARROW)
    return jax.shard_map(shards, mesh=mesh, in_specs=in_specs, out_specs=out_specs, check_vma=False)
```

```python
import functools

import jax
import jax.numpy as jnp
from jax import lax
from jax.experimental import pallas as pl
from jax.experimental.pallas import tpu as pltpu
from jax.sharding import PartitionSpec as P

D = 3200
TILE_SIDE = 32
TILE_ROWS = 256
HALF = 128
COLS = 512
PAD = 16
STEP = 256
F32 = jnp.float32
BF16 = jnp.bfloat16
WIDE, NARROW = "wide", "narrow"
(
    SENT,
    HIGH,
    OWN,
    THEIRS,
    MINE,
    BOTH,
    ALL,
    FIRST,
    NEAR,
    CAME,
    FAR,
    SECOND,
    FAR_CAME,
    NEAR_CAME,
    ACROSS,
    ACT,
    FAR_ACT,
    NEAR_ACT,
    FAR_ACT_END,
    NEAR_VALUE,
    ACTS,
    VALUE,
    PART,
    SUM,
    TRADED,
    KEPT,
    MOVED,
    PLACED,
    REST,
    HITS,
    POS,
) = range(31)


def bit_reversed(bits):
    return [sum(((p >> b) & 1) << (bits - 1 - b) for b in range(bits)) for p in range(1 << bits)]


def swap(value, axis, mask):
    count = lax.axis_size(axis)
    return lax.ppermute(value, axis, [(i, i ^ mask) for i in range(count)])


def merge_kernel(patch_ref, order_ref, *refs):
    merged_refs, stats_ref = refs[:-1], refs[-1]
    mixed = jnp.dot(patch_ref[...], order_ref[...], preferred_element_type=F32)
    total = jnp.zeros((1, HALF), F32)
    squares = jnp.zeros((1, HALF), F32)
    for slot in range(4):
        part = mixed[:, slot * HALF : (slot + 1) * HALF]
        total += jnp.sum(part, axis=0, keepdims=True)
        squares += jnp.sum(part * part, axis=0, keepdims=True)
    stats_ref[0:1, :] = total
    stats_ref[1:2, :] = squares
    for tile, merged_ref in enumerate(merged_refs):

        @pl.when(pl.program_id(0) // 2 == tile)
        def _():
            for slot in range(4):
                merged_ref[0, slot] = mixed[:, slot * HALF : (slot + 1) * HALF].astype(BF16)


def merge(patches):
    columns, width = patches.shape
    steps = width // COLS
    side = TILE_SIDE // 2
    source = lax.broadcasted_iota(jnp.int32, (COLS, COLS), 0)
    target = lax.broadcasted_iota(jnp.int32, (COLS, COLS), 1)
    slot = target // HALF
    row = target % HALF
    wanted = (
        (row // side) * (4 * side) + (slot // 2) * (2 * side) + (row % side) * 2 + slot % 2
    )
    order = (source == wanted).astype(BF16)

    def tile_spec(tile):
        return pl.BlockSpec(
            (1, 4, columns, HALF), lambda i: (jnp.clip(i - 2 * tile, 0, 1), 0, 0, 0)
        )

    tiles = steps // 2
    out = pl.pallas_call(
        merge_kernel,
        grid=(steps,),
        in_specs=[
            pl.BlockSpec((columns, COLS), lambda i: (0, i)),
            pl.BlockSpec((COLS, COLS), lambda i: (0, 0)),
        ],
        out_specs=[tile_spec(tile) for tile in range(tiles)]
        + [pl.BlockSpec((2, HALF), lambda i: (0, i))],
        out_shape=[jax.ShapeDtypeStruct((2, 4, columns, HALF), BF16)] * tiles
        + [jax.ShapeDtypeStruct((2, steps * HALF), F32)],
        compiler_params=pltpu.CompilerParams(vmem_limit_bytes=24 * 1024 * 1024),
    )(patches, order)
    return out[:-1], out[-1]


def call(kernel, grid, in_specs, out_specs, out_shape, scratch_shapes=(), scalars=0, flops=1):
    return pl.pallas_call(
        kernel,
        grid_spec=pltpu.PrefetchScalarGridSpec(
            num_scalar_prefetch=scalars,
            grid=grid,
            in_specs=in_specs,
            out_specs=out_specs,
            scratch_shapes=scratch_shapes,
        ),
        out_shape=out_shape,
        cost_estimate=pl.CostEstimate(flops=flops, bytes_accessed=1, transcendentals=0),
        compiler_params=pltpu.CompilerParams(vmem_limit_bytes=24 * 1024 * 1024),
    )


def like(rows, width):
    return jax.ShapeDtypeStruct((rows, width), BF16)


def norm_kernel(half_ref, merged_ref, mean_ref, scale_ref, gain_ref, shift_ref, out_ref):
    for slot in range(4):
        values = merged_ref[0, slot].astype(F32)
        gain, shift = gain_ref[:, slot : slot + 1], shift_ref[:, slot : slot + 1]
        result = (values - mean_ref[...]) * scale_ref[...] * gain + shift
        out_ref[slot] = result.astype(BF16)


def norm(merged, mean, scale, gain, shift, tile, halves):
    columns = merged.shape[2]
    out = call(
        norm_kernel,
        (len(halves),),
        [
            pl.BlockSpec((1, 4, columns, HALF), lambda i, h: (h[i], 0, 0, 0)),
            pl.BlockSpec((1, HALF), lambda i, h: (0, h[i] + 2 * tile)),
            pl.BlockSpec((1, HALF), lambda i, h: (0, h[i] + 2 * tile)),
            pl.BlockSpec((columns, 4), lambda i, h: (0, 0)),
            pl.BlockSpec((columns, 4), lambda i, h: (0, 0)),
        ],
        pl.BlockSpec((4, columns, HALF), lambda i, h: (0, 0, i)),
        jax.ShapeDtypeStruct((4, columns, len(halves) * HALF), BF16),
        scalars=1,
    )(jnp.stack(halves).astype(jnp.int32), merged, mean, scale, gain, shift)
    return [out.reshape(-1, len(halves) * HALF)]


def turn_kernel(first_ref, flat_ref, out_ref):
    out_ref[...] = flat_ref[...].T


def turn(flat, near):
    depth, hidden = flat.shape
    step = 256
    half = hidden // 2 // step
    return call(
        turn_kernel,
        (2 * half,),
        [pl.BlockSpec((depth, step), lambda i, n: (0, (i // half + n[0]) % 2 * half + i % half))],
        pl.BlockSpec((step, depth), lambda i, n: (i, 0)),
        like(hidden, depth),
        scalars=1,
    )(near, flat)


def whole(kernel, out_shape, scratch_shapes=(), scalars=0, count=0):
    specs = [pl.BlockSpec(memory_space=pltpu.SMEM)] * scalars
    specs += [pl.BlockSpec(memory_space=pltpu.VMEM)] * count
    return pl.pallas_call(
        kernel,
        in_specs=specs,
        out_specs=[pl.BlockSpec(memory_space=pltpu.VMEM)] * len(out_shape),
        out_shape=out_shape,
        scratch_shapes=scratch_shapes,
        cost_estimate=pl.CostEstimate(flops=1, bytes_accessed=1, transcendentals=0),
        compiler_params=pltpu.CompilerParams(vmem_limit_bytes=24 * 1024 * 1024),
    )


def product_kernel(half, start, weight_ref, *refs):
    tile_refs, out_ref, rows_ref = refs[:-2], refs[-2], refs[-1]
    for i, tile_ref in enumerate(tile_refs):
        columns = slice(half * HALF, (half + 1) * HALF)
        rows_ref[:, i * HALF : (i + 1) * HALF] = tile_ref[:, columns]
    rows = out_ref.shape[0]
    step = STEP if rows % STEP == 0 else rows
    for row in range(0, rows, step):
        weight = weight_ref[start + row : start + row + step, :]
        out = jnp.dot(weight, rows_ref[...], preferred_element_type=F32)
        out_ref[row : row + step, :] = out.astype(BF16)


def product(weight, tiles, half, start, rows):
    width = len(tiles) * HALF
    return whole(
        functools.partial(product_kernel, half, start),
        [like(rows, width)],
        [pltpu.VMEM((weight.shape[1], width), BF16)],
        count=1 + len(tiles),
    )(weight, *[tile[0] for tile in tiles])[0]


def products_kernel(weight_ref, *refs):
    tile_refs, (near_ref, far_ref, own_ref, rows_ref) = refs[:-4], refs[-4:]
    width = len(tile_refs) * HALF
    for i, tile_ref in enumerate(tile_refs):
        place = slice(i * HALF, (i + 1) * HALF)
        rows_ref[:, place] = tile_ref[:, :HALF]
        rows_ref[:, slice(width + i * HALF, width + (i + 1) * HALF)] = tile_ref[:, HALF:]
    half = near_ref.shape[0]
    step = STEP
    for row in range(0, 2 * half, step):
        some = slice(row, row + step)
        out = jnp.dot(weight_ref[some, :], rows_ref[...], preferred_element_type=F32).astype(BF16)
        own_ref[some, :] = out[:, width:]
        if row < half:
            near_ref[some, :] = out[:, :width]
        else:
            far_ref[row - half : row - half + step, :] = out[:, :width]


def products(weight, tiles):
    rows, depth = weight.shape
    width = len(tiles) * HALF
    return whole(
        products_kernel,
        [like(rows // 2, width), like(rows // 2, width), like(rows, width)],
        [pltpu.VMEM((depth, 2 * width), BF16)],
        count=1 + len(tiles),
    )(weight, *[tile[0] for tile in tiles])


def add_kernel(start, one_ref, other_ref, out_ref):
    rows = out_ref.shape[0]
    one = one_ref[start : start + rows, :].astype(F32)
    out_ref[...] = (one + other_ref[...].astype(F32)).astype(BF16)


def add(one, other, start=0):
    kernel = functools.partial(add_kernel, start)
    return whole(kernel, [like(*other.shape)], count=2)(one, other)[0]


def activate_kernel(one_ref, two_ref, three_ref, bias_ref, out_ref):
    rows = one_ref.shape[0]
    step = rows // 4
    for i in range(4):
        some = slice(i * step, (i + 1) * step)
        total = one_ref[some, :].astype(F32) + two_ref[some, :].astype(F32)
        total = total + three_ref[some, :].astype(F32) + bias_ref[some, :]
        out_ref[some, :] = (0.5 * total * (1.0 + lax.erf(total * 0.5**0.5))).astype(BF16)
    if out_ref.shape[0] > rows:
        out_ref[rows:, :] = jnp.zeros((out_ref.shape[0] - rows, out_ref.shape[1]), BF16)


def activated_sum(one, two, three, bias, pad):
    rows, width = one.shape
    return whole(activate_kernel, [like(rows + pad, width)], count=4)(one, two, three, bias)[0]


def second_kernel(place_ref, own_weight_ref, other_weight_ref, own_ref, near_ref, far_ref, end_ref, keep_ref, send_ref, units_ref):
    half = own_weight_ref.shape[1] // 2
    rows = own_weight_ref.shape[0]
    near_at = place_ref[0] * half

    @pl.when(place_ref[1] == 1)
    def _():
        units_ref[pl.ds(near_at, half), :] = own_ref[:half, :]
        units_ref[pl.ds(half - near_at, half), :] = far_ref[:half, :]

    @pl.when(place_ref[1] == 0)
    def _():
        units_ref[pl.ds(near_at, half), :] = near_ref[:half, :]
        units_ref[pl.ds(half - near_at, half), :] = end_ref[:half, :]

    cut = keep_ref.shape[1]
    for i, ref in enumerate((own_weight_ref, other_weight_ref)):
        for row in range(0, rows, STEP):
            out = jnp.dot(ref[row : row + STEP, :], units_ref[...], preferred_element_type=F32)
            some = slice(i * rows + row, i * rows + row + STEP)
            keep_ref[some, :] = out[:, :cut].astype(BF16)
            send_ref[some, :] = out[:, cut:].astype(BF16)


def second_product_of(place, weights, own, near, far, end):
    rows, depth = weights[0].shape
    width = own.shape[1]
    return whole(
        second_kernel,
        [like(2 * rows, width // 2)] * 2,
        [pltpu.VMEM((depth, width), BF16)],
        scalars=1,
        count=6,
    )(place, *weights, own, near, far, end)


def near_kernel(place_ref, own_weight_ref, other_weight_ref, own_ref, near_ref, value_ref, units_ref):
    half = units_ref.shape[0]
    rows = own_weight_ref.shape[0]

    @pl.when(place_ref[1] == 1)
    def _():
        units_ref[...] = own_ref[:half, :]

    @pl.when(place_ref[1] == 0)
    def _():
        units_ref[...] = near_ref[:half, :]

    columns = pl.ds(pl.multiple_of(place_ref[0] * half, HALF), half)
    for i, ref in enumerate((own_weight_ref, other_weight_ref)):
        for row in range(0, rows, STEP):
            weight = ref[row : row + STEP, columns]
            out = jnp.dot(weight, units_ref[...], preferred_element_type=F32)
            value_ref[i * rows + row : i * rows + row + STEP, :] = out


def near_product_of(place, weights, own, near):
    rows, depth = weights[0].shape
    width = near.shape[1]
    return whole(
        near_kernel,
        [jax.ShapeDtypeStruct((2 * rows, width), F32)],
        [pltpu.VMEM((depth // 2, width), BF16)],
        scalars=1,
        count=4,
    )(place, *weights, own, near)[0]


def far_kernel(place_ref, own_weight_ref, other_weight_ref, far_ref, end_ref, value_ref, keep_ref, send_ref, units_ref):
    half = units_ref.shape[0]
    rows = own_weight_ref.shape[0]

    @pl.when(place_ref[1] == 1)
    def _():
        units_ref[...] = far_ref[:half, :]

    @pl.when(place_ref[1] == 0)
    def _():
        units_ref[...] = end_ref[:half, :]

    cut = keep_ref.shape[1]
    columns = pl.ds(pl.multiple_of(half - place_ref[0] * half, HALF), half)
    for i, ref in enumerate((own_weight_ref, other_weight_ref)):
        for row in range(0, rows, STEP):
            some = slice(i * rows + row, i * rows + row + STEP)
            weight = ref[row : row + STEP, columns]
            out = jnp.dot(weight, units_ref[...], preferred_element_type=F32) + value_ref[some, :]
            keep_ref[some, :] = out[:, :cut].astype(BF16)
            send_ref[some, :] = out[:, cut:].astype(BF16)


def far_product_of(place, weights, far, end, value):
    rows, depth = weights[0].shape
    width = far.shape[1]
    return whole(
        far_kernel,
        [like(2 * rows, width // 2)] * 2,
        [pltpu.VMEM((depth // 2, width), BF16)],
        scalars=1,
        count=5,
    )(place, *weights, far, end, value)


def cut_kernel(one_ref, other_ref, keep_ref, send_ref):
    total = (one_ref[...].astype(F32) + other_ref[...].astype(F32)).astype(BF16)
    cut = keep_ref.shape[1]
    keep_ref[...] = total[:, :cut]
    send_ref[...] = total[:, cut:]


def cut_sum(one, other):
    rows, width = one.shape
    return whole(cut_kernel, [like(rows, width // 2)] * 2, count=2)(one, other)


def finish_kernel(start, one_ref, two_ref, bias_ref, out_ref):
    some = slice(start, start + out_ref.shape[0])
    total = one_ref[some, :].astype(F32) + two_ref[some, :].astype(F32)
    out_ref[...] = (total + bias_ref[...]).astype(BF16)


def finish(one, two, bias, half):
    rows = bias.shape[0]
    kernel = functools.partial(finish_kernel, half * rows)
    return whole(kernel, [like(rows, one.shape[1])], count=3)(one, two, bias)[0]


def shards(
    patches,
    ln_gain,
    ln_bias,
    first_weight,
    first_bias,
    second_weight,
    second_bias,
    text_embeds,
    vis_pos,
):
    wide = lax.axis_size(WIDE)
    narrow = lax.axis_size(NARROW)
    wide_bits = wide.bit_length() - 1
    narrow_bits = narrow.bit_length() - 1
    line = wide // 2
    wide_at = lax.axis_index(WIDE)
    narrow_at = lax.axis_index(NARROW)
    side_at = wide_at % 2
    line_at = wide_at // 2
    columns = patches.shape[0]
    hidden = first_weight.shape[2]
    features = second_weight.shape[0]
    tiles = patches.shape[1] // (4 * TILE_ROWS)
    prompt_rows = text_embeds.shape[1]
    depth = 4 * columns
    block = hidden // line

    merged, stats = merge(patches)
    other_bias = swap(second_bias, WIDE, 1)
    stats = stats + swap(stats, WIDE, 1)
    early = features // 2 // 16 * 16
    gain = ln_gain.astype(F32).T
    shift = ln_bias.astype(F32).T
    second_early = second_weight[:early]
    stats, second_early, other_bias, gain, shift = lax.optimization_barrier(
        (stats, second_early, other_bias, gain, shift)
    )
    for bit in range(1, wide_bits):
        stats = stats + swap(stats, WIDE, 1 << bit)
    entries = 4.0 * D
    row_mean = stats[0] / entries
    row_var = stats[1] / entries - row_mean * row_mean
    inverse = lax.rsqrt(row_var + 1e-05)
    def normed(tile, halves):
        return norm(merged[tile], row_mean[None, :], inverse[None, :], gain, shift, tile, halves)

    if line == 4:
        starts = [(line_at // 2 ^ i) * (hidden // 2) for i in range(2)]
    else:
        starts = [(line_at ^ i) * (hidden // line) for i in bit_reversed(wide_bits - 1)]
    block = hidden // len(starts)
    flat = first_weight.reshape(depth, hidden)
    own_bias = lax.dynamic_slice_in_dim(first_bias, starts[0], block, 0).astype(F32)[:, None]
    out_bias = [bias.astype(F32)[:, None] for bias in (second_bias, other_bias)]

    text_rows = narrow * prompt_rows - vis_pos.shape[0]
    first_row = narrow_at * prompt_rows
    grid = jnp.arange(prompt_rows, dtype=jnp.int32)[None, :]
    moves = {tile: [] for tile in range(tiles)}
    for tile in range(tiles):
        for step in range(1 - narrow, narrow):
            pairs = []
            for source in range(narrow):
                target = source + step
                low = (source * tiles + tile) * TILE_ROWS
                if (
                    0 <= target < narrow
                    and low < (target + 1) * prompt_rows
                    and low + text_rows + TILE_ROWS > target * prompt_rows
                ):
                    pairs.append((source, target))
            if pairs:
                moves[tile].append((step, pairs))
    groups = [(t,) for t in range(tiles)]

    tile_order = bit_reversed(narrow_bits)
    outward = [(x, 2 + x) for x in (0, 1)] + [(6 + x, 4 + x) for x in (0, 1)]
    inward = [(b, a) for a, b in outward]
    middle = [(2 + x, 4 + x) for x in (0, 1)] + [(4 + x, 2 + x) for x in (0, 1)]
    is_middle = (line_at == 1) | (line_at == 2)
    place_at = jnp.stack([line_at // 2 % 2, is_middle.astype(jnp.int32)]).astype(jnp.int32)
    have, joined = {}, set()

    def put(key, value, flying=False):
        have[key] = value
        joined.discard(key)
        if not flying:
            joined.add(key)

    def fly(key, value, axis, pairs):
        if isinstance(pairs, int):
            pairs = [(i, i ^ pairs) for i in range(lax.axis_size(axis))]
        put(key, lax.ppermute(value, axis, pairs), True)
        put((SENT, key), value)

    def sync(needs):
        joined.update(needs)
        keys = [k for k in have if k in joined]
        have.update(zip(keys, lax.optimization_barrier([have[k] for k in keys])))
        for key in keys:
            if key[0] == SENT:
                del have[key]

    def hops(key, tile, stage):
        if stage == HIGH:
            return [(key, 0, narrow // 2, tile)]
        base = 0 if stage == OWN else narrow // 2
        found, result = [base], []
        for bit in reversed(range(narrow_bits - 1)):
            result += [(key, d, d + (1 << bit), tile) for d in found]
            found += [d + (1 << bit) for d in found]
        return result

    row_parts = 1

    def of(key, tile, stage):
        return [
            (key, to, tile, part)
            for key, _, to, tile in hops(key, tile, stage)
            for part in range(row_parts)
        ]

    def norm_step(key, tile):
        theirs, mine = 1 - side_at, side_at
        halves = {THEIRS: [theirs], MINE: [mine], BOTH: [theirs, mine]}[key]
        for part, value in enumerate(normed(tile, halves)):
            put((key, 0, tile, part), value)

    def gather_step(key, tile, stage):
        for key, origin, to, tile in hops(key, tile, stage):
            for part in range(row_parts):
                fly((key, to, tile, part), have[key, origin, tile, part], NARROW, origin ^ to)

    def pieces_of(key, tile):
        return [[have[key, d, tile, part] for part in range(row_parts)] for d in tile_order]

    def drop(tile):
        for key in [key for key in have if len(key) == 4 and key[2] == tile]:
            del have[key]

    def send_theirs(tile, part):
        key = BOTH if tile else THEIRS
        pieces = pieces_of(key, tile)
        if part == ALL:
            sent = product(have[FIRST,], pieces, 0, 0, hidden)
        else:
            sent = product(have[FIRST,], pieces, 0, 0 if part == NEAR else block, block)
        put((THEIRS, part, tile), sent)

    def fly_theirs(tile, part):
        if tile < tiles:
            fly((CAME, part, tile), have.pop((THEIRS, part, tile)), WIDE, 1)

    def send_and_keep(tile):
        if line == 4:
            near, far, own = products(have[FIRST,], pieces_of(BOTH, tile))
            put((THEIRS, NEAR, tile), near)
            put((THEIRS, FAR, tile), far)
            put((OWN, tile), own)
            drop(tile)
        else:
            send_theirs(tile, ALL)
            fly_theirs(tile, ALL)
            keep_mine(tile)

    def keep_mine(tile):
        key = BOTH if tile else MINE
        own = product(have[FIRST,], pieces_of(key, tile), 1 if tile else 0, 0, hidden)
        put((OWN, tile), own)
        drop(tile)

    def second_weights():
        return [second_weight, have[SECOND,]]

    def second_columns(at):
        parts = [lax.dynamic_slice_in_dim(part, at, block, 1) for part in second_weights()]
        return jnp.concatenate(parts, axis=0)

    def join_second():
        parts = [have.pop((SECOND, 0)), have.pop((SECOND, 1))]
        put((SECOND,), jnp.concatenate(parts, axis=0))

    def far_ready(tile):
        if tile:
            fly_theirs(tile, NEAR)
        put((FAR, tile), add(have[OWN, tile], have.pop((CAME, FAR, tile)), block))

    def near_ready(tile):
        fly_theirs(tile + 1, FAR)
        put((NEAR, tile), add(have.pop((OWN, tile)), have.pop((CAME, NEAR, tile))))

    def far_out(tile):
        if tile < tiles:
            fly((FAR_CAME, tile), have[FAR, tile], WIDE, outward)

    def near_out(tile):
        fly((NEAR_CAME, tile), have[NEAR, tile], WIDE, outward)

    def across(tile):
        far = add(have.pop((FAR, tile)), have.pop((FAR_CAME, tile)))
        fly((ACROSS, tile), far, WIDE, middle)

    def activate(tile):
        terms = [have.pop((key, tile)) for key in (NEAR, NEAR_CAME, ACROSS)]
        act = activated_sum(*terms, own_bias, PAD if tile == tiles - 1 else 0)
        put((ACT, tile), act)
        fly((FAR_ACT, tile), act, WIDE, middle)
        fly((NEAR_ACT, tile), act, WIDE, inward)

    def far_in(tile):
        fly((FAR_ACT_END, tile), have[FAR_ACT, tile], WIDE, inward)

    def near_product(tile):
        terms = [have[ACT, tile], have[NEAR_ACT, tile]]
        put((NEAR_VALUE, tile), near_product_of(place_at, second_weights(), *terms))

    def second_product(group):
        tile = group[0]
        if line == 4 and tile == tiles - 1:
            far, end = have.pop((FAR_ACT, tile)), have.pop((FAR_ACT_END, tile))
            value = have.pop((NEAR_VALUE, tile))
            out = far_product_of(place_at, second_weights(), far, end, value)
            del have[ACT, tile], have[NEAR_ACT, tile]
        elif line == 4:
            names = (ACT, NEAR_ACT, FAR_ACT, FAR_ACT_END)
            terms = [have.pop((name, tile)) for name in names]
            out = second_product_of(place_at, second_weights(), *terms)
        else:
            units = jnp.concatenate(have.pop((ACTS, tile)), axis=0)
            second = jnp.concatenate([second_columns(s) for s in starts], axis=1)
            value = jnp.dot(second, units, preferred_element_type=F32).astype(BF16)
            cut = value.shape[1] // 2
            out = value[:, :cut], value[:, cut:]
        put((VALUE, group), out[0])
        fly((PART, group), out[1], NARROW, 1)

    def halve(bit):
        def step(tile):
            if bit == 1:
                came = have.pop((CAME, ALL, tile))
                total = have.pop((OWN, tile)).astype(F32) + came.astype(F32)
            else:
                total = have.pop((SUM, tile)).astype(F32) + have.pop((PART, tile)).astype(F32)
            total = total.astype(BF16)
            cut = total.shape[0] // 2
            put((SUM, tile), total[:cut])
            put((PART, tile), swap(total[cut:], WIDE, 1 << bit))

        return step

    def double(bit):
        def step(tile):
            if bit == wide_bits - 1:
                total = have.pop((SUM, tile)).astype(F32) + have.pop((PART, tile)).astype(F32)
                act = jax.nn.gelu(total + own_bias, approximate=False).astype(BF16)
                put((ACTS, tile), [act])
            acts = have[ACTS, tile]
            put((ACTS, tile), acts + [swap(act, WIDE, 1 << bit) for act in acts])

        return step

    def narrow_step(group, bit):
        value, send = cut_sum(have[VALUE, group], have[PART, group])
        put((VALUE, group), value)
        fly((PART, group), send, NARROW, 1 << bit)

    def trade(group):
        done = finish(have[VALUE, group], have[PART, group], out_bias[1], 1)
        fly((TRADED, group), done, WIDE, 1)

    def keep(group):
        put((KEPT, group), finish(have.pop((VALUE, group)), have.pop((PART, group)), out_bias[0], 0))

    def steps_of(group):
        pairs = {}
        for tile in group:
            for step, some in moves[tile]:
                pairs[step] = sorted(set(pairs.get(step, []) + some))
        return dict(sorted(pairs.items()))

    def halo(group):
        whole = jnp.concatenate([have.pop((KEPT, group)), have.pop((TRADED, group))], axis=1)
        for step, pairs in steps_of(group).items():
            if step:
                fly((MOVED, step, group), whole, NARROW, pairs)
            else:
                put((MOVED, step, group), whole)

    def place(group):
        keys = [(MOVED, step, group) for step in steps_of(group)]
        moved = jnp.concatenate([have.pop(key) for key in keys], axis=1)
        more = jnp.dot(moved, have.pop((HITS, group)), preferred_element_type=F32)
        put((PLACED,), (have[PLACED,].astype(F32) + more).astype(BF16))

    def late_second():
        fly((SECOND, 1), second_weight[early:], WIDE, 1)

    def order_first():
        if line == 4:
            put((FIRST,), turn(have[FIRST,], place_at[:1]))
        else:
            cut = [lax.dynamic_slice_in_dim(have[FIRST,], s, block, 1) for s in starts]
            put((FIRST,), jnp.concatenate(cut, axis=1).T)

    def spot_of(step, tile, half):
        whose = narrow_at - step
        at = (jnp.clip(whose, 0, narrow - 1) * tiles + tile) * TILE_ROWS + half * HALF
        spot = lax.dynamic_slice_in_dim(have[POS,], at, HALF, 0) - first_row
        return jnp.where((whose >= 0) & (whose < narrow), spot, -1)

    def clear_marked():
        marked = jnp.zeros((prompt_rows,), bool)
        for group in groups:
            steps = sorted({step for tile in group for step, _ in moves[tile]})
            spots = [
                spot_of(step, tile, half)
                for step in steps
                for half in (side_at, 1 - side_at)
                for tile in group
            ]
            found = jnp.concatenate(spots)[:, None] == grid
            marked |= jnp.any(found, axis=0)
            put((HITS, group), found.astype(BF16))
        put((PLACED,), jnp.where(marked[None, :], jnp.zeros((), BF16), have[PLACED,]))

    put((FIRST,), flat)
    put((PLACED,), text_embeds)
    put((POS,), vis_pos)
    fly((SECOND, 0), second_early, WIDE, 1)

    events = []

    def at(time, needs, step, *args):
        events.append((time, len(events), needs, step, args))

    parts = [FAR, NEAR] if line == 4 else [ALL]
    nothing = lambda: None
    at(19, [], norm_step, THEIRS, 0)
    at(20, [], gather_step, THEIRS, 0, HIGH)
    at(20.1, [], gather_step, THEIRS, 0, OWN)
    at(21, [], norm_step, MINE, 0)
    at(22, [], order_first)
    at(30, of(THEIRS, 0, HIGH), gather_step, THEIRS, 0, REST)
    at(31, [], gather_step, MINE, 0, HIGH)
    at(31.1, [], norm_step, BOTH, 1)
    at(31.2, [], gather_step, BOTH, 1, HIGH)
    needs = of(THEIRS, 0, OWN) + of(THEIRS, 0, REST) + [(SECOND, 0)]
    at(34, needs, send_theirs, 0, parts[0])
    at(34.1, [], fly_theirs, 0, parts[0])
    at(42, of(MINE, 0, HIGH), gather_step, MINE, 0, OWN)
    at(42.1, [], gather_step, MINE, 0, REST)
    if line == 4:
        at(42.2, [], send_theirs, 0, NEAR)
        at(42.3, [], fly_theirs, 0, NEAR)
    at(45, of(MINE, 0, OWN) + of(MINE, 0, REST), keep_mine, 0)
    for tile in range(2, tiles):
        at(45.1 + 0.1 * tile, [], norm_step, BOTH, tile)
    tick = 19.5
    for tile in range(1, tiles):
        arrived = 65 + tick * (tile - 1) + 0.4
        if tile == 1:
            at(arrived, [], gather_step, BOTH, 1, OWN)
        at(arrived, of(BOTH, tile, HIGH), gather_step, BOTH, tile, REST)
        if tile + 1 < tiles:
            at(arrived + 0.1, [], gather_step, BOTH, tile + 1, HIGH)
            at(arrived + 0.2, [], gather_step, BOTH, tile + 1, OWN)
        needs = of(BOTH, tile, OWN) + of(BOTH, tile, REST)
        at(68 if tile == 1 else 65 + tick * tile - 0.1, needs, nothing)
        at(68.1 if tile == 1 else 65 + tick * (2 * tile - 2) + 1, [], send_and_keep, tile)
    last = 65 + tick * (2 * tiles - 1)
    at(65 + 3 * tick + 3, [], clear_marked)
    at(last + 0.2, [], late_second)
    for tile in range(tiles):
        if line == 4:
            a = 65 + tick * (2 * tile + 1)
            b = a + tick
            if tile == 0:
                at(a - tick, [(CAME, FAR, 0)], far_ready, 0)
                at(a - tick, [], far_out, 0)
            at(a, [(CAME, NEAR, tile)], near_ready, tile)
            at(a + 0.1, [(FAR_CAME, tile)], near_out, tile)
            at(a + 0.1, [], across, tile)
            if tile + 1 < tiles:
                at(b, [(CAME, FAR, tile + 1)], far_ready, tile + 1)
            at(b + 0.1, [(NEAR_CAME, tile)], far_out, tile + 1)
            at(b + 0.2, [(ACROSS, tile)], activate, tile)
            at(b + tick + 0.3, [(FAR_ACT, tile), (NEAR_ACT, tile)], far_in, tile)
            at(b + 2 * tick + 0.3, [(FAR_ACT_END, tile)], nothing)
        else:
            base = 74 + 37 * tile
            for i, bit in enumerate(range(1, wide_bits)):
                needs = [(PART, tile)] if i else [(CAME, ALL, tile)]
                at(base + 8 * i, needs, halve(bit), tile)
            for i, bit in enumerate(reversed(range(1, wide_bits))):
                needs = [] if i else [(PART, tile)]
                at(base + 35 + 8 * i, needs, double(bit), tile)
    done = last + 3 * tick + 0.4
    at(done - 2 * tick + 4, [(SECOND, 1)], join_second)
    if line == 4:
        at(done - 12, [], near_product, tiles - 1)
    for i, group in enumerate(groups):
        if line == 4 and tiles == 4:
            times = (
                (-34, -19, -6, 5, 13),
                (-33, -18.9, 3, 12.5, 21),
                (-18.8, 1, 12, 20.5, 28),
                (0, 4, 20, 27, 31),
            )[i]
        else:
            times = (10 * i, 10 * i + 1, 10 * i + 5, 10 * i + 6, 10 * i + 7)
        times = [done + time for time in times]
        at(times[0], [], second_product, group)
        for bit in range(1, narrow_bits):
            at(times[1] + 0.1 * bit, [(PART, group)], narrow_step, group, bit)
        at(times[2], [(PART, group)], trade, group)
        at(times[2] + 0.1, [], keep, group)
        at(times[3], [(TRADED, group)], halo, group)
        flown = [(MOVED, step, group) for step in steps_of(group) if step]
        at(times[4], flown, place, group)
    for _, _, needs, step, args in sorted(events, key=lambda e: e[:2]):
        sync(needs)
        step(*args)
    return have[PLACED,]


def solution(mesh):
    in_specs = (
        P(WIDE, NARROW),
        P(None, WIDE),
        P(None, WIDE),
        P(None, WIDE, NARROW),
        P(NARROW),
        P(WIDE, NARROW),
        P(WIDE),
        P(WIDE, NARROW),
        P(),
    )
    out_specs = P(WIDE, NARROW)
    return jax.shard_map(shards, mesh=mesh, in_specs=in_specs, out_specs=out_specs, check_vma=False)
```
